32 devices in a mesh: row: 8 (over y, x, core), col: 4 (over z).
Axes of the slice: x: 2, y: 2, z: 4, core: 2. Of those that a mesh axis runs over, the one named last changes fastest.
Arguments:
- cholesky_vectors: float32 [64, 512, 512], P(('row', 'col')), as said below
- factor: float32 [512, 2048], P(('row', 'col')), may hold values from -0.25 to 0.25
- core_weights: float32 [64, 2048], P(('row', 'col')), may hold values from -0.75 to 0.75
Outputs:
- core_gradient: float32 [64, 2048], P(('row', 'col'))
- factor_gradient: float32 [512, 2048], P('row', 'col')
The draws below stay inside these ranges and needn't reach their ends.
Inputs may be any that keep to these rules, and one draw needn't show every extreme that they name: Each cholesky_vectors[P] is symmetric.
All inputs are finite; a program needn't handle non-finite values.
Results may differ from the reference program's by a relative error of at most 0.0001.
Values sent between devices are 32-bit elements; how exact they have to be, the bound alone decides.
No kernel may reach another device: no remote copies, remote signals or barrier semaphores. Data moves between devices by JAX's collectives and lax.ppermute only.
A program may use at most 384 MiB of HBM per device.

```python
import jax
import jax.numpy as jnp
from jax import lax

N = 512
R = 2048
NAUX = 64


def draw_cholesky_vectors(key, part):
    first = jax.random.fold_in(jax.random.fold_in(key, 11), 0)
    base = jax.random.normal(first, (NAUX, N, N), jnp.float32)
    return (base + jnp.swapaxes(base, 1, 2)) * 0.7071


def block_scale(own_key, shape, shards, low, high):
    def one(dim, parts):
        draws = jax.random.uniform(jax.random.fold_in(jax.random.fold_in(own_key, 6), dim), (parts,), jnp.float32, low / len(shards), high / len(shards))
        return jnp.repeat(jnp.exp(draws), shape[dim] // parts).reshape((-1,) + (1,) * (len(shape) - dim - 1))

    factor_of = one(*shards[0])
    for cut in shards[1:]:
        factor_of = factor_of * one(*cut)
    return factor_of


def bell_draw(own_key, extent, deviation, bound, pieces=(), held_as=jnp.bfloat16):
    entries = deviation * jax.random.normal(own_key, extent, jnp.float32)
    if pieces:
        entries = entries * block_scale(own_key, extent, pieces, -0.22, 0.18)
    return jnp.clip(entries, -bound, bound).astype(held_as)


def setup_inputs(seed: int = 0) -> dict:
    key_list = jax.random.split(jax.random.key(seed), 4)
    return {
        "cholesky_vectors": draw_cholesky_vectors(jax.random.fold_in(key_list[3], 71), 0),
        "factor": bell_draw(key_list[1], (N, R), N ** -0.5, 0.25, ((0, 32),), jnp.float32),
        "core_weights": bell_draw(key_list[2], (NAUX, R), NAUX ** -0.5, 0.75, ((0, 32),), jnp.float32),
    }


def reference(cholesky_vectors, factor, core_weights):
    high = lax.Precision.HIGHEST
    gram = jnp.dot(factor.T, factor, precision=high, preferred_element_type=jnp.float32)
    correlation_sq = gram * gram
    core_gram = jnp.dot(core_weights.T, core_weights, precision=high, preferred_element_type=jnp.float32)

    def one_vector(carry, inputs):
        matrix, weights = inputs
        adjoint = jnp.dot(matrix, factor, precision=high, preferred_element_type=jnp.float32)
        projected = jnp.sum(factor * adjoint, axis=0)
        return carry + adjoint * weights[None, :], projected

    start = jnp.zeros((N, R), jnp.float32)
    adjoint_sum, projection = lax.scan(one_vector, start, (cholesky_vectors, core_weights))
    core_gradient = jnp.dot(core_weights, correlation_sq, precision=high, preferred_element_type=jnp.float32) - projection
    factor_gradient = 4.0 * (jnp.dot(factor, gram * core_gram, precision=high, preferred_element_type=jnp.float32) - adjoint_sum)
    return core_gradient, factor_gradient
```

```python
import jax
import jax.numpy as jnp
from jax import lax
from jax.sharding import PartitionSpec as P

HIGH = lax.Precision.HIGH


def dot(a, b, dims):
    return lax.dot_general(a, b, (dims, ((), ())), precision=HIGH, preferred_element_type=jnp.float32)


def on_device(vectors, factor, weights):
    rows = lax.axis_size("row")
    cols = lax.axis_size("col")
    r = lax.axis_index("row")
    c = lax.axis_index("col")
    own, orbitals = vectors.shape[:2]
    rank = factor.shape[1]
    row_width = rank // rows
    col_width = rank // cols
    orb = orbitals // rows

    blocks = [
        lax.all_to_all(vectors[v], "row", split_axis=0, concat_axis=0, tiled=True) for v in range(own)
    ]
    x = lax.all_gather(factor, ("row", "col"), axis=0, tiled=True)
    z = lax.all_gather(weights, ("row", "col"), axis=0, tiled=True)

    x_rows = lax.dynamic_slice_in_dim(x, r * orb, orb, 0)
    x_left = lax.dynamic_slice_in_dim(x, r * row_width, row_width, 1)
    x_right = lax.dynamic_slice_in_dim(x, c * col_width, col_width, 1)
    z_right = lax.dynamic_slice_in_dim(z, c * col_width, col_width, 1)
    z_group = lax.dynamic_slice_in_dim(z.reshape(rows, cols, own, rank), c, 1, 1)[:, 0]

    gram = dot(x_left, x, ((0,), (0,)))
    z_left = lax.dynamic_slice_in_dim(z_group, r * row_width, row_width, 2)
    core = dot(z_left.reshape(rows * own, row_width), gram * gram, ((1,), (0,))).reshape(rows, own, rank)

    mixed = dot(x, x_right, ((0,), (0,))) * dot(z, z_right, ((0,), (0,)))
    factor_part = dot(x_rows, mixed, ((1,), (0,)))

    adjoint_sum = jnp.zeros((orb, rank), jnp.float32)
    projections = []
    for v in range(own):
        adjoint = dot(blocks[v], x, ((1,), (0,))).reshape(rows, orb, rank)
        projections.append(jnp.sum(adjoint * x_rows[None], axis=1))
        adjoint_sum = adjoint_sum + jnp.sum(adjoint * z_group[:, v, None, :], axis=0)
    core = core - jnp.stack(projections, axis=1)

    core = lax.all_to_all(core.reshape(rows * own, rank), "row", split_axis=0, concat_axis=0, tiled=True)
    core_gradient = jnp.sum(core.reshape(rows, own, rank), axis=0)
    parts = adjoint_sum.reshape(orb, cols, col_width).swapaxes(0, 1)
    parts = lax.all_to_all(parts, "col", split_axis=0, concat_axis=0, tiled=True)
    factor_gradient = 4.0 * (factor_part - jnp.sum(parts, axis=0))
    return core_gradient, factor_gradient


def solution(mesh):
    placed = (P(("row", "col"), None, None), P(("row", "col"), None), P(("row", "col"), None))
    return jax.shard_map(
        on_device,
        mesh=mesh,
        in_specs=placed,
        out_specs=(P(("row", "col"), None), P("row", "col")),
        check_vma=False,
    )
```

```python
import jax
import jax.numpy as jnp
from jax import lax
from jax.sharding import PartitionSpec as P

HIGH = lax.Precision.HIGH


def dot(a, b, dims):
    return lax.dot_general(a, b, (dims, ((), ())), precision=HIGH, preferred_element_type=jnp.float32)


def place(pieces, order):
    whole = jnp.zeros((len(pieces),) + pieces[0].shape, pieces[0].dtype)
    for piece, index in zip(pieces, order):
        whole = lax.dynamic_update_index_in_dim(whole, piece, index, 0)
    return whole


def gather_blocks(block, rows, cols, r, c):
    pieces = [block]
    for k in range(1, cols):
        pieces.append(lax.ppermute(block, "col", [(j, (j + k) % cols) for j in range(cols)]))
    line = place(pieces, [(c + cols - k) % cols for k in range(cols)])
    masks = list(range(0, rows, 2))
    even = [line] + [lax.ppermute(line, "row", [(i, i ^ m) for i in range(rows)]) for m in masks[1:]]
    odd = [lax.ppermute(piece, "row", [(i, i ^ 1) for i in range(rows)]) for piece in even]
    return place(even + odd, [r ^ m for m in masks] + [r ^ m ^ 1 for m in masks])


def on_device(vectors, factor, weights):
    rows = lax.axis_size("row")
    cols = lax.axis_size("col")
    r = lax.axis_index("row")
    c = lax.axis_index("col")
    own, orbitals = vectors.shape[:2]
    rank = factor.shape[1]
    row_width = rank // rows
    col_width = rank // cols
    orb = orbitals // rows

    blocks = [
        lax.all_to_all(vectors[v], "row", split_axis=0, concat_axis=0, tiled=True) for v in range(own)
    ]
    held = factor.shape[0]
    whole = gather_blocks(jnp.concatenate([factor, weights], axis=0), rows, cols, r, c)
    x = whole[:, :, :held].reshape(orbitals, rank)
    z = whole[:, :, held:].reshape(rows * cols * own, rank)

    x_rows = lax.dynamic_slice_in_dim(x, r * orb, orb, 0)
    x_left = lax.dynamic_slice_in_dim(x, r * row_width, row_width, 1)
    x_right = lax.dynamic_slice_in_dim(x, c * col_width, col_width, 1)
    z_right = lax.dynamic_slice_in_dim(z, c * col_width, col_width, 1)
    z_group = lax.dynamic_slice_in_dim(z.reshape(rows, cols, own, rank), c, 1, 1)[:, 0]

    gram = dot(x_left, x, ((0,), (0,)))
    z_left = lax.dynamic_slice_in_dim(z_group, r * row_width, row_width, 2)
    core = dot(z_left.reshape(rows * own, row_width), gram * gram, ((1,), (0,))).reshape(rows, own, rank)

    mixed = dot(x, x_right, ((0,), (0,))) * dot(z, z_right, ((0,), (0,)))
    factor_part = dot(x_rows, mixed, ((1,), (0,)))

    adjoint_sum = jnp.zeros((orb, rank), jnp.float32)
    projections = []
    for v in range(own):
        adjoint = dot(blocks[v], x, ((1,), (0,))).reshape(rows, orb, rank)
        projections.append(jnp.sum(adjoint * x_rows[None], axis=1))
        adjoint_sum = adjoint_sum + jnp.sum(adjoint * z_group[:, v, None, :], axis=0)
    core = core - jnp.stack(projections, axis=1)

    core = lax.all_to_all(core.reshape(rows * own, rank), "row", split_axis=0, concat_axis=0, tiled=True)
    core_gradient = jnp.sum(core.reshape(rows, own, rank), axis=0)
    parts = adjoint_sum.reshape(orb, cols, col_width).swapaxes(0, 1)
    parts = lax.all_to_all(parts, "col", split_axis=0, concat_axis=0, tiled=True)
    factor_gradient = 4.0 * (factor_part - jnp.sum(parts, axis=0))
    return core_gradient, factor_gradient


def solution(mesh):
    placed = (P(("row", "col"), None, None), P(("row", "col"), None), P(("row", "col"), None))
    return jax.shard_map(
        on_device,
        mesh=mesh,
        in_specs=placed,
        out_specs=(P(("row", "col"), None), P("row", "col")),
        check_vma=False,
    )
```

```python
import functools

import jax
import jax.numpy as jnp
from jax import lax
from jax.experimental import pallas as pl
from jax.experimental.pallas import tpu as pltpu
from jax.sharding import PartitionSpec as P

F32 = jnp.float32
BF16 = jnp.bfloat16
VMEM_LIMIT = 56 * 1024 * 1024


def split(a):
    high = a.astype(BF16)
    return high, (a - high.astype(F32)).astype(BF16)


def dot3(a, b):
    both = functools.partial(jnp.dot, preferred_element_type=F32)
    return both(a[0], b[0]) + both(a[0], b[1]) + both(a[1], b[0])


def whole_spec():
    return pl.BlockSpec(memory_space=pltpu.VMEM)


def width_of(extent, most):
    return most if extent % most == 0 else extent


def assemble_kernel(dims, index_ref, *refs):
    rows, cols, own, held, rank = dims
    pieces, (high_ref, low_ref, mine_ref, group_ref, all_ref, core_ref) = refs[:rows], refs[rows:]
    r = index_ref[0]
    c = index_ref[1]
    packed = pieces[0].shape[1] - rank
    per_row = rank // packed
    orb = cols * held

    for slot in range(rows):
        piece = pieces[slot]
        row = lax.bitwise_xor(r, slot)
        for k in range(cols):
            line = lax.rem(c + cols - k, cols)
            values = piece[k * held : (k + 1) * held, :rank]
            high, low = split(values)
            start = pl.multiple_of(row * orb + line * held, held)
            high_ref[pl.ds(start, held), :] = high
            low_ref[pl.ds(start, held), :] = low
            if slot == 0:
                mine_ref[pl.ds(pl.multiple_of(line * held, held), held), :] = values
            for v in range(own):
                for j in range(per_row):
                    part = piece[pl.ds(k * held + v * per_row + j, 1), rank:]
                    span = slice(j * packed, (j + 1) * packed)
                    all_ref[pl.ds((slot * cols + k) * own + v, 1), span] = part
                    if k == 0:
                        group_ref[pl.ds(row * own + v, 1), span] = part

    row_width = rank // rows
    block = pl.ds(pl.multiple_of(r * row_width, row_width), row_width)
    left = (high_ref[:, block].T, low_ref[:, block].T)
    weights = split(group_ref[:, block])
    step = width_of(rank, 512)
    for n in range(0, rank, step):
        gram = dot3(left, (high_ref[:, n : n + step], low_ref[:, n : n + step]))
        core_ref[:, n : n + step] = dot3(weights, split(gram * gram))


def adjoint_kernel(dims, vectors_ref, high_ref, low_ref, mine_ref, group_ref, core_ref, out_ref, sum_ref, left_high, left_low, held_ref):
    rows, cols, own, held, rank = dims
    orb = cols * held

    @pl.when(pl.program_id(0) == 0)
    def _():
        left_high[...], left_low[...] = split(vectors_ref[...])

    held_ref[...] = dot3((left_high[...], left_low[...]), (high_ref[...], low_ref[...]))
    mine = mine_ref[...]
    total = jnp.zeros_like(mine)
    for vector in range(rows * own):
        adjoint = held_ref[vector * orb : (vector + 1) * orb, :]
        out_ref[vector : vector + 1, :] = core_ref[vector : vector + 1, :] - jnp.sum(adjoint * mine, axis=0, keepdims=True)
        total = total + adjoint * group_ref[vector : vector + 1, :]
    sum_ref[...] = total


def factor_kernel(dims, index_ref, high_ref, low_ref, mine_ref, all_ref, out_ref):
    rows, cols, own, held, rank = dims
    c = index_ref[1]
    col_width = rank // cols
    block = pl.ds(pl.multiple_of(c * col_width, col_width), col_width)
    left = (high_ref[:, block].T, low_ref[:, block].T)
    weight_left = split(all_ref[:, block].T)
    mine = split(mine_ref[...].T)
    total = jnp.zeros((col_width, mine[0].shape[1]), F32)
    step = width_of(rank, 512)
    for n in range(0, rank, step):
        gram = dot3(left, (high_ref[:, n : n + step], low_ref[:, n : n + step]))
        weight = dot3(weight_left, split(all_ref[:, n : n + step]))
        total = total + dot3(split(gram * weight), (mine[0][n : n + step], mine[1][n : n + step]))
    out_ref[...] = total.T


def params():
    return pltpu.CompilerParams(vmem_limit_bytes=VMEM_LIMIT)


def in_order(pieces, order):
    whole = jnp.zeros((len(pieces),) + pieces[0].shape, pieces[0].dtype)
    for piece, index in zip(pieces, order):
        whole = lax.dynamic_update_index_in_dim(whole, piece, index, 0)
    return whole


def on_device(vectors, factor, weights):
    rows = lax.axis_size("row")
    cols = lax.axis_size("col")
    r = lax.axis_index("row")
    c = lax.axis_index("col")
    own, orbitals = vectors.shape[:2]
    held, rank = factor.shape
    orb = orbitals // rows
    col_width = rank // cols
    count = rows * own
    dims = (rows, cols, own, held, rank)

    blocks = lax.all_to_all(vectors, "row", split_axis=1, concat_axis=0, tiled=True)
    blocks = blocks.reshape(count * orb, orbitals)

    block = jnp.concatenate([factor, weights.reshape(held, own * rank // held)], axis=1)
    line = [block]
    for k in range(1, cols):
        line.append(lax.ppermute(block, "col", [(j, (j + k) % cols) for j in range(cols)]))
    line = jnp.concatenate(line, axis=0)
    line, blocks = lax.optimization_barrier((line, blocks))
    pieces = [line]
    for m in range(2, rows, 2):
        pieces.append(lax.ppermute(line, "row", [(i, i ^ m) for i in range(rows)]))
    pieces = [
        part
        for piece in pieces
        for part in (piece, lax.ppermute(piece, "row", [(i, i ^ 1) for i in range(rows)]))
    ]

    index = jnp.stack([r, c]).astype(jnp.int32)
    shape = jax.ShapeDtypeStruct
    high, low, mine, group, every, core = pl.pallas_call(
        functools.partial(assemble_kernel, dims),
        out_shape=(
            shape((orbitals, rank), BF16),
            shape((orbitals, rank), BF16),
            shape((orb, rank), F32),
            shape((count, rank), F32),
            shape((rows * cols * own, rank), F32),
            shape((count, rank), F32),
        ),
        in_specs=[pl.BlockSpec(memory_space=pltpu.SMEM)] + [whole_spec()] * rows,
        out_specs=(whole_spec(),) * 6,
        compiler_params=params(),
        cost_estimate=pl.CostEstimate(
            flops=6 * orbitals * rank * rank // rows, bytes_accessed=8 * orbitals * rank, transcendentals=0
        ),
        name="assemble",
    )(index, *pieces)

    step = width_of(rank, 256)
    core, adjoint_sum = pl.pallas_call(
        functools.partial(adjoint_kernel, dims),
        grid=(rank // step,),
        out_shape=(shape((count, rank), F32), shape((orb, rank), F32)),
        in_specs=[
            whole_spec(),
            pl.BlockSpec((orbitals, step), lambda i: (0, i)),
            pl.BlockSpec((orbitals, step), lambda i: (0, i)),
            pl.BlockSpec((orb, step), lambda i: (0, i)),
            pl.BlockSpec((count, step), lambda i: (0, i)),
            pl.BlockSpec((count, step), lambda i: (0, i)),
        ],
        out_specs=(pl.BlockSpec((count, step), lambda i: (0, i)), pl.BlockSpec((orb, step), lambda i: (0, i))),
        scratch_shapes=[
            pltpu.VMEM((count * orb, orbitals), BF16),
            pltpu.VMEM((count * orb, orbitals), BF16),
            pltpu.VMEM((count * orb, step), F32),
        ],
        compiler_params=params(),
        cost_estimate=pl.CostEstimate(
            flops=6 * count * orb * orbitals * rank, bytes_accessed=8 * orbitals * rank, transcendentals=0
        ),
        name="adjoint",
    )(blocks, high, low, mine, group, core)

    factor_part = pl.pallas_call(
        functools.partial(factor_kernel, dims),
        out_shape=shape((orb, col_width), F32),
        in_specs=[pl.BlockSpec(memory_space=pltpu.SMEM)] + [whole_spec()] * 4,
        out_specs=whole_spec(),
        compiler_params=params(),
        cost_estimate=pl.CostEstimate(
            flops=6 * orbitals * rank * col_width, bytes_accessed=8 * orbitals * rank, transcendentals=0
        ),
        name="factor",
    )(index, high, low, mine, every)

    core = lax.all_to_all(core, "row", split_axis=0, concat_axis=0, tiled=True)
    core_gradient = jnp.sum(core.reshape(rows, own, rank), axis=0)
    parts = adjoint_sum.reshape(orb, cols, col_width).swapaxes(0, 1)
    parts = lax.all_to_all(parts, "col", split_axis=0, concat_axis=0, tiled=True)
    factor_gradient = 4.0 * (factor_part - jnp.sum(parts, axis=0))
    return core_gradient, factor_gradient


def solution(mesh):
    placed = (P(("row", "col"), None, None), P(("row", "col"), None), P(("row", "col"), None))
    return jax.shard_map(
        on_device,
        mesh=mesh,
        in_specs=placed,
        out_specs=(P(("row", "col"), None), P("row", "col")),
        check_vma=False,
    )
```

```python
import functools

import jax
import jax.numpy as jnp
from jax import lax
from jax.experimental import pallas as pl
from jax.experimental.pallas import tpu as pltpu
from jax.sharding import PartitionSpec as P

F32 = jnp.float32
BF16 = jnp.bfloat16
VMEM_LIMIT = 56 * 1024 * 1024


def split(a):
    high = a.astype(BF16)
    return high, (a - high.astype(F32)).astype(BF16)


def dot3(a, b):
    both = functools.partial(jnp.dot, preferred_element_type=F32)
    return both(a[0], b[0]) + both(a[0], b[1]) + both(a[1], b[0])


def whole_spec():
    return pl.BlockSpec(memory_space=pltpu.VMEM)


def width_of(extent, most):
    return most if extent % most == 0 else extent


def assemble_kernel(dims, index_ref, *refs):
    rows, cols, own, held, rank = dims
    pieces, (high_ref, low_ref, mine_ref, group_ref, all_ref, core_ref, *more) = refs[: 2 * cols], refs[2 * cols :]
    rows_ref = more[0] if more else None
    r = index_ref[0]
    c = index_ref[1]
    packed = pieces[0].shape[1] - rank
    per_row = rank // packed
    orb = cols * held

    for slot in range(2 * cols):
        piece = pieces[slot]
        line = lax.rem(c + cols - slot // 2, cols)
        for k in range(rows // 2):
            row = lax.bitwise_xor(r, 2 * k + slot % 2)
            values = piece[k * held : (k + 1) * held, :rank]
            start = row * orb + line * held
            if held % 16 == 0:
                start = pl.multiple_of(start, held)
                high_ref[pl.ds(start, held), :], low_ref[pl.ds(start, held), :] = split(values)
            else:
                for i in range(held):
                    rows_ref[pl.ds(start + i, 1), :] = values[i : i + 1]
            if slot % 2 == 0 and k == 0:
                if held % 8 == 0:
                    mine_ref[pl.ds(pl.multiple_of(line * held, held), held), :] = values
                else:
                    for i in range(held):
                        mine_ref[pl.ds(line * held + i, 1), :] = values[i : i + 1]
            for v in range(own):
                for j in range(per_row):
                    part = piece[pl.ds(k * held + v * per_row + j, 1), rank:]
                    span = slice(j * packed, (j + 1) * packed)
                    all_ref[pl.ds((slot * (rows // 2) + k) * own + v, 1), span] = part
                    if slot < 2:
                        group_ref[pl.ds(row * own + v, 1), span] = part
    if held % 16 != 0:
        high_ref[...], low_ref[...] = split(rows_ref[...])

    row_width = rank // rows
    block = pl.ds(pl.multiple_of(r * row_width, row_width), row_width)
    left = (high_ref[:, block].T, low_ref[:, block].T)
    weights = split(group_ref[:, block])
    step = width_of(rank, 512)
    for n in range(0, rank, step):
        gram = dot3(left, (high_ref[:, n : n + step], low_ref[:, n : n + step]))
        core_ref[:, n : n + step] = dot3(weights, split(gram * gram))


def adjoint_kernel(dims, vectors_ref, high_ref, low_ref, mine_ref, group_ref, core_ref, out_ref, sum_ref, left_high, left_low, held_ref):
    rows, cols, own, held, rank = dims
    orb = cols * held

    @pl.when(pl.program_id(0) == 0)
    def _():
        left_high[...], left_low[...] = split(vectors_ref[...])

    held_ref[...] = dot3((left_high[...], left_low[...]), (high_ref[...], low_ref[...]))
    mine = mine_ref[...]
    total = jnp.zeros_like(mine)
    for vector in range(rows * own):
        adjoint = held_ref[vector * orb : (vector + 1) * orb, :]
        projection = jnp.sum(adjoint * mine, axis=0, keepdims=True)
        out_ref[vector // own, vector % own : vector % own + 1, :] = core_ref[vector : vector + 1, :] - projection
        total = total + adjoint * group_ref[vector : vector + 1, :]
    sum_ref[0] = total


def factor_kernel(dims, index_ref, high_ref, low_ref, mine_ref, all_ref, out_ref):
    rows, cols, own, held, rank = dims
    c = index_ref[1]
    col_width = rank // cols
    block = pl.ds(pl.multiple_of(c * col_width, col_width), col_width)
    left = (high_ref[:, block].T, low_ref[:, block].T)
    weight_left = split(all_ref[:, block].T)
    mine = split(mine_ref[...].T)
    total = jnp.zeros((col_width, mine[0].shape[1]), F32)
    step = width_of(rank, 512)
    for n in range(0, rank, step):
        gram = dot3(left, (high_ref[:, n : n + step], low_ref[:, n : n + step]))
        weight = dot3(weight_left, split(all_ref[:, n : n + step]))
        total = total + dot3(split(gram * weight), (mine[0][n : n + step], mine[1][n : n + step]))
    out_ref[...] = total.T


def params():
    return pltpu.CompilerParams(vmem_limit_bytes=VMEM_LIMIT)


def in_order(pieces, order):
    whole = jnp.zeros((len(pieces),) + pieces[0].shape, pieces[0].dtype)
    for piece, index in zip(pieces, order):
        whole = lax.dynamic_update_index_in_dim(whole, piece, index, 0)
    return whole


def on_device(vectors, factor, weights):
    rows = lax.axis_size("row")
    cols = lax.axis_size("col")
    r = lax.axis_index("row")
    c = lax.axis_index("col")
    own, orbitals = vectors.shape[:2]
    held, rank = factor.shape
    orb = orbitals // rows
    col_width = rank // cols
    count = rows * own
    dims = (rows, cols, own, held, rank)

    blocks = vectors.reshape(own, rows, orb, orbitals).swapaxes(0, 1)
    blocks = lax.all_to_all(lax.optimization_barrier(blocks), "row", split_axis=0, concat_axis=0, tiled=True)
    blocks = blocks.reshape(count * orb, orbitals)

    block = jnp.concatenate([factor, weights.reshape(held, own * rank // held)], axis=1)
    square = [block]
    for m in range(2, rows, 2):
        square.append(lax.ppermute(block, "row", [(i, i ^ m) for i in range(rows)]))
    square = jnp.concatenate(square, axis=0)
    below, above = [square], [square]
    for _ in range(1, cols):
        below.append(lax.ppermute(below[-1], "col", [(j, j + 1) for j in range(cols - 1)]))
        above.append(lax.ppermute(above[-1], "col", [(j + 1, j) for j in range(cols - 1)]))
    slabs = [square] + [jnp.where(c >= k, below[k], above[cols - k]) for k in range(1, cols)]
    pieces = [
        part
        for slab in slabs
        for part in (slab, lax.ppermute(slab, "row", [(i, i ^ 1) for i in range(rows)]))
    ]

    index = jnp.stack([r, c]).astype(jnp.int32)
    shape = jax.ShapeDtypeStruct
    high, low, mine, group, every, core = pl.pallas_call(
        functools.partial(assemble_kernel, dims),
        out_shape=(
            shape((orbitals, rank), BF16),
            shape((orbitals, rank), BF16),
            shape((orb, rank), F32),
            shape((count, rank), F32),
            shape((rows * cols * own, rank), F32),
            shape((count, rank), F32),
        ),
        in_specs=[pl.BlockSpec(memory_space=pltpu.SMEM)] + [whole_spec()] * (2 * cols),
        out_specs=(whole_spec(),) * 6,
        scratch_shapes=[] if held % 16 == 0 else [pltpu.VMEM((orbitals, rank), F32)],
        compiler_params=params(),
        cost_estimate=pl.CostEstimate(
            flops=6 * orbitals * rank * rank // rows, bytes_accessed=8 * orbitals * rank, transcendentals=0
        ),
        name="assemble",
    )(index, *pieces)

    step = width_of(col_width, 256)
    per_col = col_width // step
    core, adjoint_sum = pl.pallas_call(
        functools.partial(adjoint_kernel, dims),
        grid=(rank // step,),
        out_shape=(shape((rows, own, rank), F32), shape((cols, orb, col_width), F32)),
        in_specs=[
            whole_spec(),
            pl.BlockSpec((orbitals, step), lambda i: (0, i)),
            pl.BlockSpec((orbitals, step), lambda i: (0, i)),
            pl.BlockSpec((orb, step), lambda i: (0, i)),
            pl.BlockSpec((count, step), lambda i: (0, i)),
            pl.BlockSpec((count, step), lambda i: (0, i)),
        ],
        out_specs=(
            pl.BlockSpec((rows, own, step), lambda i: (0, 0, i)),
            pl.BlockSpec((1, orb, step), lambda i: (i // per_col, 0, i % per_col)),
        ),
        scratch_shapes=[
            pltpu.VMEM((count * orb, orbitals), BF16),
            pltpu.VMEM((count * orb, orbitals), BF16),
            pltpu.VMEM((count * orb, step), F32),
        ],
        compiler_params=params(),
        cost_estimate=pl.CostEstimate(
            flops=6 * count * orb * orbitals * rank, bytes_accessed=8 * orbitals * rank, transcendentals=0
        ),
        name="adjoint",
    )(blocks, high, low, mine, group, core)

    factor_part = pl.pallas_call(
        functools.partial(factor_kernel, dims),
        out_shape=shape((orb, col_width), F32),
        in_specs=[pl.BlockSpec(memory_space=pltpu.SMEM)] + [whole_spec()] * 4,
        out_specs=whole_spec(),
        compiler_params=params(),
        cost_estimate=pl.CostEstimate(
            flops=6 * orbitals * rank * col_width, bytes_accessed=8 * orbitals * rank, transcendentals=0
        ),
        name="factor",
    )(index, high, low, mine, every)

    core = lax.all_to_all(core, "row", split_axis=0, concat_axis=0, tiled=True)
    core_gradient = jnp.sum(core, axis=0)
    parts = lax.all_to_all(adjoint_sum, "col", split_axis=0, concat_axis=0, tiled=True)
    factor_gradient = 4.0 * (factor_part - jnp.sum(parts, axis=0))
    return core_gradient, factor_gradient


def solution(mesh):
    placed = (P(("row", "col"), None, None), P(("row", "col"), None), P(("row", "col"), None))
    return jax.shard_map(
        on_device,
        mesh=mesh,
        in_specs=placed,
        out_specs=(P(("row", "col"), None), P("row", "col")),
        check_vma=False,
    )
```

```python
import functools

import jax
import jax.numpy as jnp
from jax import lax
from jax.experimental import pallas as pl
from jax.experimental.pallas import tpu as pltpu
from jax.sharding import PartitionSpec as P

F32 = jnp.float32
BF16 = jnp.bfloat16
VMEM_LIMIT = 32 * 1024 * 1024


def split(a):
    high = a.astype(BF16)
    return high, (a - high.astype(F32)).astype(BF16)


def dot3(a, b):
    both = functools.partial(jnp.dot, preferred_element_type=F32)
    return both(a[0], b[0]) + both(a[0], b[1]) + both(a[1], b[0])


def width_of(extent, most):
    return most if extent % most == 0 else extent


def put_rows(ref, start, values, unit):
    height = values.shape[0]
    if height % unit == 0:
        ref[pl.ds(pl.multiple_of(start, unit), height), :] = values
    else:
        for i in range(height):
            ref[pl.ds(start + i, 1), :] = values[i : i + 1]


def assemble_kernel(dims, places, index_ref, *refs):
    rows, cols, own, held, rank = dims
    pieces = refs[: len(places)]
    high_ref, low_ref, mine_ref, group_ref, all_ref, core_ref, *more = refs[len(places) :]
    r = index_ref[0]
    c = index_ref[1]
    packed = pieces[0].shape[1] - rank
    per_row = rank // packed
    orb = cols * held

    seen = 0
    for piece, (mask, first, many) in zip(pieces, places):
        row = lax.bitwise_xor(r, mask)
        for k in range(many):
            line = lax.rem(c + cols - (first + k), cols)
            values = piece[k * held : (k + 1) * held, :rank]
            start = row * orb + line * held
            if more:
                put_rows(more[0], start, values, 8)
            else:
                high, low = split(values)
                put_rows(high_ref, start, high, 16)
                put_rows(low_ref, start, low, 16)
            if mask == 0:
                put_rows(mine_ref, line * held, values, 8)
            for v in range(own):
                for j in range(per_row):
                    part = piece[pl.ds(k * held + v * per_row + j, 1), rank:]
                    span = slice(j * packed, (j + 1) * packed)
                    all_ref[pl.ds(seen + v, 1), span] = part
                    if first + k == 0:
                        group_ref[pl.ds(row * own + v, 1), span] = part
            seen += own
    if more:
        high_ref[...], low_ref[...] = split(more[0][...])

    row_width = rank // rows
    block = pl.ds(pl.multiple_of(r * row_width, row_width), row_width)
    left = (high_ref[:, block].T, low_ref[:, block].T)
    weights = split(group_ref[:, block])
    step = width_of(rank, 512)
    for n in range(0, rank, step):
        gram = dot3(left, (high_ref[:, n : n + step], low_ref[:, n : n + step]))
        core = dot3(weights, split(gram * gram))
        for i in range(rows * own):
            core_ref[i // own, i % own : i % own + 1, n : n + step] = core[i : i + 1]


def adjoint_kernel(dims, v, index_ref, vector_ref, high_ref, low_ref, mine_ref, group_ref, core_ref, *refs):
    rows, cols, own, held, rank = dims
    before = refs[0] if v else None
    out_ref, sum_ref, left_high, left_low, even_ref, odd_ref = refs[1:] if v else refs
    orb = cols * held
    c = index_ref[1]
    col_width = rank // cols
    step = even_ref.shape[1]
    per_col = col_width // step
    left_high[...], left_low[...] = split(vector_ref[...])
    stages = (even_ref, odd_ref)

    def finish(n):
        span = slice(n * step, (n + 1) * step)
        offset = slice((n % per_col) * step, (n % per_col + 1) * step)
        slot = lax.rem(n // per_col + cols - c, cols)
        mine = mine_ref[:, span]
        total = before[slot, :, offset] if v else jnp.zeros_like(mine)
        for i in range(rows):
            adjoint = stages[n % 2][i * orb : (i + 1) * orb, :]
            projection = jnp.sum(adjoint * mine, axis=0, keepdims=True)
            for w in range(own):
                core = core_ref[i, w : w + 1, span]
                out_ref[i, w : w + 1, span] = core - projection if w == v else core
            total = total + adjoint * group_ref[i * own + v : i * own + v + 1, span]
        sum_ref[slot, :, offset] = total

    for n in range(rank // step):
        span = slice(n * step, (n + 1) * step)
        stages[n % 2][...] = dot3((left_high[...], left_low[...]), (high_ref[:, span], low_ref[:, span]))
        if n:
            finish(n - 1)
    finish(rank // step - 1)


def factor_kernel(dims, index_ref, high_ref, low_ref, mine_ref, all_ref, out_ref):
    rows, cols, own, held, rank = dims
    c = index_ref[1]
    col_width = rank // cols
    block = pl.ds(pl.multiple_of(c * col_width, col_width), col_width)
    left = (high_ref[:, block].T, low_ref[:, block].T)
    weight_left = split(all_ref[:, block].T)
    mine = split(mine_ref[...].T)
    total = jnp.zeros((col_width, mine[0].shape[1]), F32)
    step = width_of(rank, 512)
    for n in range(0, rank, step):
        gram = dot3(left, (high_ref[:, n : n + step], low_ref[:, n : n + step]))
        weight = dot3(weight_left, split(all_ref[:, n : n + step]))
        total = total + dot3(split(gram * weight), (mine[0][n : n + step], mine[1][n : n + step]))
    out_ref[...] = total.T


def kernel_call(body, name, index, operands, outs, scratch, flops):
    whole = pl.BlockSpec(memory_space=pltpu.VMEM)
    moved = sum(a.size * a.dtype.itemsize for a in operands)
    return pl.pallas_call(
        body,
        out_shape=tuple(pltpu.VMEM(*out) for out in outs),
        in_specs=[pl.BlockSpec(memory_space=pltpu.SMEM)] + [whole] * len(operands),
        out_specs=(whole,) * len(outs),
        scratch_shapes=[pltpu.VMEM(*held) for held in scratch],
        compiler_params=pltpu.CompilerParams(vmem_limit_bytes=VMEM_LIMIT),
        cost_estimate=pl.CostEstimate(flops=flops, bytes_accessed=moved, transcendentals=0),
        name=name,
    )(index, *(pltpu.with_memory_space_constraint(a, pltpu.VMEM) for a in operands))


def on_device(vectors, factor, weights):
    rows = lax.axis_size("row")
    cols = lax.axis_size("col")
    r = lax.axis_index("row")
    c = lax.axis_index("col")
    own, orbitals = vectors.shape[:2]
    held, rank = factor.shape
    orb = orbitals // rows
    col_width = rank // cols
    count = rows * own
    dims = (rows, cols, own, held, rank)
    index = jnp.stack([r, c]).astype(jnp.int32)

    def across(a, mask):
        return lax.ppermute(a, "row", [(i, i ^ mask) for i in range(rows)])

    def spread(vector):
        return lax.all_to_all(vector, "row", split_axis=0, concat_axis=0, tiled=True)

    blocks = [spread(vectors[0])]
    block = jnp.concatenate([factor, weights.reshape(held, own * rank // held)], axis=1)
    line = [block]
    for k in range(1, cols):
        line.append(lax.ppermute(block, "col", [(j, (j + k) % cols) for j in range(cols)]))
    line, blocks[0] = lax.optimization_barrier((jnp.concatenate(line, axis=0), blocks[0]))

    whole = [(line, 0, 0, cols)]
    if rows == 8:
        half = cols // 2
        one, two = across(line, 2), across(line, 4)
        whole += [(one, 2, 0, cols), (two, 4, 0, cols)]
        whole += [(across(two[: half * held], 2), 6, 0, half), (across(one[half * held :], 4), 6, half, cols - half)]
    else:
        whole += [(across(line, m), m, 0, cols) for m in range(2, rows, 2)]
    rest, _ = lax.optimization_barrier((vectors[1:], [part[0] for part in whole[1:]]))
    blocks += [spread(rest[v]) for v in range(own - 1)]
    whole += [(across(part, 1), mask + 1, first, many) for part, mask, first, many in whole]

    high, low, mine, group, every, core = kernel_call(
        functools.partial(assemble_kernel, dims, [part[1:] for part in whole]),
        "assemble",
        index,
        [part[0] for part in whole],
        [
            ((orbitals, rank), BF16),
            ((orbitals, rank), BF16),
            ((orb, rank), F32),
            ((count, rank), F32),
            ((count * cols, rank), F32),
            ((rows, own, rank), F32),
        ],
        [] if held % 16 == 0 else [((orbitals, rank), F32)],
        6 * orbitals * rank * rank // rows,
    )

    step = width_of(col_width, 256)
    total = []
    for v in range(own):
        core, *total = kernel_call(
            functools.partial(adjoint_kernel, dims, v),
            "adjoint",
            index,
            [blocks[v], high, low, mine, group, core, *total],
            [((rows, own, rank), F32), ((cols, orb, col_width), F32)],
            [((rows * orb, orbitals), BF16)] * 2 + [((rows * orb, step), F32)] * 2,
            6 * rows * orb * orbitals * rank,
        )

    (factor_part,) = kernel_call(
        functools.partial(factor_kernel, dims),
        "factor",
        index,
        [high, low, mine, every],
        [((orb, col_width), F32)],
        [],
        6 * orbitals * rank * col_width,
    )

    core = lax.all_to_all(core, "row", split_axis=0, concat_axis=0, tiled=True)
    core_gradient = jnp.sum(core, axis=0)
    parts = total[0][0]
    for k in range(1, cols):
        parts = parts + lax.ppermute(total[0][k], "col", [(j, (j + k) % cols) for j in range(cols)])
    factor_gradient = 4.0 * (factor_part - parts)
    return core_gradient, factor_gradient


def solution(mesh):
    placed = (P(("row", "col"), None, None), P(("row", "col"), None), P(("row", "col"), None))
    return jax.shard_map(
        on_device,
        mesh=mesh,
        in_specs=placed,
        out_specs=(P(("row", "col"), None), P("row", "col")),
        check_vma=False,
    )
```

```python
import functools

import jax
import jax.numpy as jnp
from jax import lax
from jax.experimental import pallas as pl
from jax.experimental.pallas import tpu as pltpu
from jax.sharding import PartitionSpec as P

F32 = jnp.float32
BF16 = jnp.bfloat16
VMEM_LIMIT = 32 * 1024 * 1024


def split(a):
    high = a.astype(BF16)
    return high, (a - high.astype(F32)).astype(BF16)


def dot3(a, b):
    both = functools.partial(jnp.dot, preferred_element_type=F32)
    return both(a[0], b[0]) + both(a[0], b[1]) + both(a[1], b[0])


def width_of(extent, most):
    return most if extent % most == 0 else extent


def put_rows(ref, start, values, unit):
    height = values.shape[0]
    if height % unit == 0:
        ref[pl.ds(pl.multiple_of(start, unit), height), :] = values
    else:
        for i in range(height):
            ref[pl.ds(start + i, 1), :] = values[i : i + 1]


def gram_kernel(dims, places, index_ref, *refs):
    rows, cols, own, held, rank = dims
    pieces = refs[: len(places)]
    high_out, low_out, mine_ref, group_ref, core_ref, factor_ref = refs[len(places) : len(places) + 6]
    high_ref, low_ref, all_ref, strip_ref, sems, *more = refs[len(places) + 6 :]
    r = index_ref[0]
    c = index_ref[1]
    packed = pieces[0].shape[1] - rank
    per_row = rank // packed
    lanes = strip_ref.shape[2]
    orb = cols * held

    seen = 0
    for piece, (mask, first, many) in zip(pieces, places):
        row = lax.bitwise_xor(r, mask)
        for k in range(many):
            line = lax.rem(c + cols - (first + k), cols)
            values = piece[k * held : (k + 1) * held, :rank]
            start = row * orb + line * held
            if more:
                put_rows(more[0], start, values, 8)
            else:
                high, low = split(values)
                put_rows(high_ref, start, high, 16)
                put_rows(low_ref, start, low, 16)
            if mask == 0:
                put_rows(mine_ref, line * held, values, 8)
        taken = many * own
        for h in range(packed // lanes):
            strip_ref[h, : many * held, :] = piece[:, rank + h * lanes : rank + (h + 1) * lanes]
            for j in range(per_row):
                at = j * packed + h * lanes
                part = strip_ref[h, pl.ds(j, taken, stride=per_row), :]
                all_ref[seen : seen + taken, at : at + lanes] = part
        if first == 0:
            for v in range(own):
                for j in range(per_row):
                    part = piece[pl.ds(v * per_row + j, 1), rank:]
                    group_ref[pl.ds(row * own + v, 1), j * packed : (j + 1) * packed] = part
        seen += taken
    if more:
        high_ref[...], low_ref[...] = split(more[0][...])
    copies = [
        pltpu.make_async_copy(high_ref, high_out, sems.at[0]),
        pltpu.make_async_copy(low_ref, low_out, sems.at[1]),
    ]
    for copy in copies:
        copy.start()

    row_width = rank // rows
    col_width = rank // cols
    row_block = pl.ds(pl.multiple_of(r * row_width, row_width), row_width)
    col_block = pl.ds(pl.multiple_of(c * col_width, col_width), col_width)
    row_left = (high_ref[:, row_block].T, low_ref[:, row_block].T)
    col_left = (high_ref[:, col_block].T, low_ref[:, col_block].T)
    row_weights = split(group_ref[:, row_block])
    col_weights = split(all_ref[:, col_block].T)
    mine = split(mine_ref[...].T)
    total = jnp.zeros((col_width, orb), F32)
    step = width_of(rank, 512)
    for n in range(0, rank, step):
        right = (high_ref[:, n : n + step], low_ref[:, n : n + step])
        gram = dot3(row_left, right)
        core_ref[:, n : n + step] = dot3(row_weights, split(gram * gram))
        mixed = dot3(col_left, right) * dot3(col_weights, split(all_ref[:, n : n + step]))
        total = total + dot3(split(mixed), (mine[0][n : n + step], mine[1][n : n + step]))
    factor_ref[...] = total.T
    for copy in copies:
        copy.wait()


def adjoint_kernel(dims, index_ref, *refs):
    rows, cols, own, held, rank = dims
    vectors = refs[:own]
    high_in, low_in, mine_ref, group_ref, core_ref, out_ref = refs[own : own + 6]
    sums = refs[own + 6 : own + 6 + cols]
    left_high, left_low, high_ref, low_ref, even_ref, odd_ref, sems = refs[own + 6 + cols :]
    orb = cols * held
    c = index_ref[1]
    col_width = rank // cols
    step = even_ref.shape[1]
    stages = (even_ref, odd_ref)
    order = [(k % cols, m) for k in range(1, cols + 1) for m in range(0, col_width, step)]
    spans = [pl.ds(pl.multiple_of(lax.rem(c + k, cols) * col_width + m, step), step) for k, m in order]

    def fetch(n):
        return (
            pltpu.make_async_copy(high_in.at[:, spans[n]], high_ref.at[n], sems.at[0, n]),
            pltpu.make_async_copy(low_in.at[:, spans[n]], low_ref.at[n], sems.at[1, n]),
        )

    for n in range(len(order)):
        for copy in fetch(n):
            copy.start()
    for v in range(own):
        part = slice(v * rows * orb, (v + 1) * rows * orb)
        left_high[part, :], left_low[part, :] = split(vectors[v][...])

    def finish(n):
        k, m = order[n]
        mine = mine_ref[:, spans[n]]
        weights = group_ref[:, spans[n]]
        core = core_ref[:, spans[n]]
        total = jnp.zeros_like(mine)
        for i in range(rows):
            for v in range(own):
                at = (v * rows + i) * orb
                vector = i * own + v
                adjoint = stages[n % 2][at : at + orb, :]
                projection = jnp.sum(adjoint * mine, axis=0, keepdims=True)
                out_ref[i, v : v + 1, spans[n]] = core[vector : vector + 1] - projection
                total = total + adjoint * weights[vector : vector + 1]
        sums[k][:, m : m + step] = total

    for n in range(len(order)):
        for copy in fetch(n):
            copy.wait()
        stages[n % 2][...] = dot3((left_high[...], left_low[...]), (high_ref[n], low_ref[n]))
        if n:
            finish(n - 1)
    finish(len(order) - 1)


VMEM_SPEC = pl.BlockSpec(memory_space=pltpu.VMEM)
HBM_SPEC = pl.BlockSpec(memory_space=pl.ANY)


def kernel_call(body, name, index, operands, specs, outs, out_specs, scratch, flops):
    return pl.pallas_call(
        body,
        out_shape=tuple(jax.ShapeDtypeStruct(*out) for out in outs),
        in_specs=[pl.BlockSpec(memory_space=pltpu.SMEM)] + specs,
        out_specs=tuple(out_specs),
        scratch_shapes=scratch,
        compiler_params=pltpu.CompilerParams(vmem_limit_bytes=VMEM_LIMIT),
        cost_estimate=pl.CostEstimate(flops=flops, bytes_accessed=8 << 20, transcendentals=0),
        name=name,
    )(index, *operands)


def in_vmem(a):
    return pltpu.with_memory_space_constraint(a, pltpu.VMEM)


def on_device(vectors, factor, weights):
    rows = lax.axis_size("row")
    cols = lax.axis_size("col")
    r = lax.axis_index("row")
    c = lax.axis_index("col")
    own, orbitals = vectors.shape[:2]
    held, rank = factor.shape
    orb = orbitals // rows
    col_width = rank // cols
    count = rows * own
    dims = (rows, cols, own, held, rank)
    index = jnp.stack([r, c]).astype(jnp.int32)

    def across(a, mask):
        return lax.ppermute(a, "row", [(i, i ^ mask) for i in range(rows)])

    def spread(vector):
        return lax.all_to_all(vector, "row", split_axis=0, concat_axis=0, tiled=True)

    blocks = [spread(vectors[0])]
    block = jnp.concatenate([factor, weights.reshape(held, own * rank // held)], axis=1)
    line = [block]
    for k in range(1, cols):
        line.append(lax.ppermute(block, "col", [(j, (j + k) % cols) for j in range(cols)]))
    line, blocks[0], vectors = lax.optimization_barrier((jnp.concatenate(line, axis=0), blocks[0], vectors))

    whole = [(line, 0, 0, cols)]
    if rows == 8:
        half = cols // 2
        one, two = across(line, 2), across(line, 4)
        whole += [(one, 2, 0, cols), (two, 4, 0, cols)]
        whole += [(across(two[: half * held], 2), 6, 0, half), (across(one[half * held :], 4), 6, half, cols - half)]
    else:
        whole += [(across(line, m), m, 0, cols) for m in range(2, rows, 2)]
    other = [(across(part, 1), mask + 1, first, many) for part, mask, first, many in whole]
    later = [vectors[v] for v in range(1, own)]
    later, _ = lax.optimization_barrier((later, [part[0] for part in other[:3]]))
    blocks += [spread(vector) for vector in later]
    whole += other

    high, low, mine, group, core, factor_part = kernel_call(
        functools.partial(gram_kernel, dims, [part[1:] for part in whole]),
        "gram",
        index,
        [in_vmem(part[0]) for part in whole],
        [VMEM_SPEC] * len(whole),
        [
            ((orbitals, rank), BF16),
            ((orbitals, rank), BF16),
            ((orb, rank), F32),
            ((count, rank), F32),
            ((count, rank), F32),
            ((orb, col_width), F32),
        ],
        [HBM_SPEC] * 2 + [VMEM_SPEC] * 4,
        [
            pltpu.VMEM((orbitals, rank), BF16),
            pltpu.VMEM((orbitals, rank), BF16),
            pltpu.VMEM((count * cols, rank), F32),
            pltpu.VMEM((own * rank // held // 128, cols * held, 128), F32),
            pltpu.SemaphoreType.DMA((2,)),
        ]
        + ([] if held % 16 == 0 else [pltpu.VMEM((orbitals, rank), F32)]),
        6 * orbitals * rank * (rank // rows + col_width),
    )

    step = width_of(col_width, 256)
    chunks = rank // step
    core, *sums = kernel_call(
        functools.partial(adjoint_kernel, dims),
        "adjoint",
        index,
        [in_vmem(part) for part in blocks] + [high, low, mine, group, core],
        [VMEM_SPEC] * own + [HBM_SPEC] * 2 + [VMEM_SPEC] * 3,
        [((rows, own, rank), F32)] + [((orb, col_width), F32)] * cols,
        [VMEM_SPEC] * (1 + cols),
        [pltpu.VMEM((count * orb, orbitals), BF16)] * 2
        + [pltpu.VMEM((chunks, orbitals, step), BF16)] * 2
        + [pltpu.VMEM((count * orb, step), F32)] * 2
        + [pltpu.SemaphoreType.DMA((2, chunks))],
        6 * count * orb * orbitals * rank,
    )

    parts = sums[0]
    for k in range(1, cols):
        parts = parts + lax.ppermute(sums[k], "col", [(j, (j + k) % cols) for j in range(cols)])
    core = lax.all_to_all(core, "row", split_axis=0, concat_axis=0, tiled=True)
    core_gradient = jnp.sum(core, axis=0)
    factor_gradient = 4.0 * (factor_part - parts)
    return core_gradient, factor_gradient


def solution(mesh):
    placed = (P(("row", "col"), None, None), P(("row", "col"), None), P(("row", "col"), None))
    return jax.shard_map(
        on_device,
        mesh=mesh,
        in_specs=placed,
        out_specs=(P(("row", "col"), None), P("row", "col")),
        check_vma=False,
    )
```

```python
import functools

import jax
import jax.numpy as jnp
from jax import lax
from jax.experimental import pallas as pl
from jax.experimental.pallas import tpu as pltpu
from jax.sharding import PartitionSpec as P

F32 = jnp.float32
BF16 = jnp.bfloat16
VMEM_LIMIT = 32 * 1024 * 1024


def split(a):
    high = a.astype(BF16)
    return high, (a - high.astype(F32)).astype(BF16)


def dot3(a, b):
    both = functools.partial(jnp.dot, preferred_element_type=F32)
    return both(a[0], b[0]) + both(a[0], b[1]) + both(a[1], b[0])


def width_of(extent, most):
    return most if extent % most == 0 else extent


def put_rows(ref, start, values, unit):
    height = values.shape[0]
    if height % unit == 0:
        ref[pl.ds(pl.multiple_of(start, unit), height), :] = values
    else:
        for i in range(height):
            ref[pl.ds(start + i, 1), :] = values[i : i + 1]


def assemble_kernel(dims, places, index_ref, *refs):
    rows, cols, own, held, rank = dims
    pieces = refs[: len(places)]
    high_ref, low_ref, mine_ref, group_ref, all_ref, core_ref, strip_ref, *more = refs[len(places) :]
    r = index_ref[0]
    c = index_ref[1]
    packed = pieces[0].shape[1] - rank
    per_row = rank // packed
    lanes = strip_ref.shape[2]
    orb = cols * held

    seen = 0
    for piece, (mask, first, many) in zip(pieces, places):
        row = lax.bitwise_xor(r, mask)
        for k in range(many):
            line = lax.rem(c + cols - (first + k), cols)
            values = piece[k * held : (k + 1) * held, :rank]
            start = row * orb + line * held
            if more:
                put_rows(more[0], start, values, 8)
            else:
                high, low = split(values)
                put_rows(high_ref, start, high, 16)
                put_rows(low_ref, start, low, 16)
            if mask == 0:
                put_rows(mine_ref, line * held, values, 8)
        taken = many * own
        for h in range(packed // lanes):
            strip_ref[h, : many * held, :] = piece[:, rank + h * lanes : rank + (h + 1) * lanes]
            for j in range(per_row):
                at = j * packed + h * lanes
                all_ref[seen : seen + taken, at : at + lanes] = strip_ref[h, pl.ds(j, taken, stride=per_row), :]
        if first == 0:
            for v in range(own):
                for j in range(per_row):
                    part = piece[pl.ds(v * per_row + j, 1), rank:]
                    group_ref[pl.ds(row * own + v, 1), j * packed : (j + 1) * packed] = part
        seen += taken
    if more:
        high_ref[...], low_ref[...] = split(more[0][...])

    row_width = rank // rows
    block = pl.ds(pl.multiple_of(r * row_width, row_width), row_width)
    left = (high_ref[:, block].T, low_ref[:, block].T)
    weights = split(group_ref[:, block])
    step = width_of(rank, 512)
    for n in range(0, rank, step):
        gram = dot3(left, (high_ref[:, n : n + step], low_ref[:, n : n + step]))
        core = dot3(weights, split(gram * gram))
        for i in range(rows * own):
            core_ref[i // own, i % own : i % own + 1, n : n + step] = core[i : i + 1]


def adjoint_kernel(dims, v, index_ref, *refs):
    rows, cols, own, held, rank = dims
    blocks = 1 if v == 0 else rows
    vector_refs = refs[:blocks]
    high_ref, low_ref, mine_ref, group_ref, core_ref, *refs = refs[blocks:]
    r = index_ref[0]
    before = refs[0] if v else None
    out_ref, sum_ref, left_high, left_low, even_ref, odd_ref = refs[1:] if v else refs
    orb = cols * held
    c = index_ref[1]
    col_width = rank // cols
    step = even_ref.shape[1]
    per_col = col_width // step
    height = rows * orb // blocks
    for i, vector_ref in enumerate(vector_refs):
        part = slice(i * height, (i + 1) * height)
        left_high[part, :], left_low[part, :] = split(vector_ref[...])
    stages = (even_ref, odd_ref)

    def finish(n):
        span = slice(n * step, (n + 1) * step)
        offset = slice((n % per_col) * step, (n % per_col + 1) * step)
        slot = lax.rem(n // per_col + cols - c, cols)
        mine = mine_ref[:, span]
        total = before[slot, :, offset] if v else jnp.zeros_like(mine)
        for i in range(rows):
            adjoint = stages[n % 2][i * orb : (i + 1) * orb, :]
            projection = jnp.sum(adjoint * mine, axis=0, keepdims=True)
            row = i if v == 0 else lax.bitwise_xor(r, i)
            for w in range(own):
                core = core_ref[row, w : w + 1, span]
                out_ref[i if v in (0, own - 1) else row, w : w + 1, span] = core - projection if w == v else core
            total = total + adjoint * group_ref[pl.ds(row * own + v, 1), span]
        sum_ref[slot, :, offset] = total

    for n in range(rank // step):
        span = slice(n * step, (n + 1) * step)
        stages[n % 2][...] = dot3((left_high[...], left_low[...]), (high_ref[:, span], low_ref[:, span]))
        if n:
            finish(n - 1)
    finish(rank // step - 1)


def factor_kernel(dims, index_ref, high_ref, low_ref, mine_ref, all_ref, out_ref):
    rows, cols, own, held, rank = dims
    c = index_ref[1]
    col_width = rank // cols
    block = pl.ds(pl.multiple_of(c * col_width, col_width), col_width)
    left = (high_ref[:, block].T, low_ref[:, block].T)
    weight_left = split(all_ref[:, block].T)
    mine = split(mine_ref[...].T)
    total = jnp.zeros((col_width, mine[0].shape[1]), F32)
    step = width_of(rank, 512)
    for n in range(0, rank, step):
        gram = dot3(left, (high_ref[:, n : n + step], low_ref[:, n : n + step]))
        weight = dot3(weight_left, split(all_ref[:, n : n + step]))
        total = total + dot3(split(gram * weight), (mine[0][n : n + step], mine[1][n : n + step]))
    out_ref[...] = total.T


def kernel_call(body, name, index, operands, outs, scratch, flops):
    whole = pl.BlockSpec(memory_space=pltpu.VMEM)
    moved = sum(a.size * a.dtype.itemsize for a in operands)
    return pl.pallas_call(
        body,
        out_shape=tuple(pltpu.VMEM(*out) for out in outs),
        in_specs=[pl.BlockSpec(memory_space=pltpu.SMEM)] + [whole] * len(operands),
        out_specs=(whole,) * len(outs),
        scratch_shapes=[pltpu.VMEM(*held) for held in scratch],
        compiler_params=pltpu.CompilerParams(vmem_limit_bytes=VMEM_LIMIT),
        cost_estimate=pl.CostEstimate(flops=flops, bytes_accessed=moved, transcendentals=0),
        name=name,
    )(index, *(pltpu.with_memory_space_constraint(a, pltpu.VMEM) for a in operands))


def on_device(vectors, factor, weights):
    rows = lax.axis_size("row")
    cols = lax.axis_size("col")
    r = lax.axis_index("row")
    c = lax.axis_index("col")
    own, orbitals = vectors.shape[:2]
    held, rank = factor.shape
    orb = orbitals // rows
    col_width = rank // cols
    count = rows * own
    dims = (rows, cols, own, held, rank)
    index = jnp.stack([r, c]).astype(jnp.int32)

    def across(a, mask):
        return lax.ppermute(a, "row", [(i, i ^ mask) for i in range(rows)])

    def spread(vector):
        return lax.all_to_all(vector, "row", split_axis=0, concat_axis=0, tiled=True)

    blocks = [spread(vectors[0])]
    block = jnp.concatenate([factor, weights.reshape(held, own * rank // held)], axis=1)
    line = [block]
    for k in range(1, cols):
        line.append(lax.ppermute(block, "col", [(j, (j + k) % cols) for j in range(cols)]))
    line, blocks[0], vectors = lax.optimization_barrier((jnp.concatenate(line, axis=0), blocks[0], vectors))

    def pick(v, mask):
        return lax.dynamic_slice(vectors, (v, (r ^ mask) * orb, 0), (1, orb, orbitals))[0]

    later = [[pick(v, mask) for mask in range(rows)] for v in range(1, own)]
    whole = [(line, 0, 0, cols)]
    if rows == 8:
        half = cols // 2
        one, two = across(line, 2), across(line, 4)
        give, take, later = lax.optimization_barrier((two[: half * held], one[half * held :], later))
        whole += [(one, 2, 0, cols), (two, 4, 0, cols)]
        whole += [(across(give, 2), 6, 0, half), (across(take, 4), 6, half, cols - half)]
    else:
        whole += [(across(line, m), m, 0, cols) for m in range(2, rows, 2)]
    later = [[parts[0]] + [across(parts[m], m) for m in range(1, rows)] for parts in later]
    blocks = [[blocks[0]]] + later
    whole += [(across(part, 1), mask + 1, first, many) for part, mask, first, many in whole]

    high, low, mine, group, every, core = kernel_call(
        functools.partial(assemble_kernel, dims, [part[1:] for part in whole]),
        "assemble",
        index,
        [part[0] for part in whole],
        [
            ((orbitals, rank), BF16),
            ((orbitals, rank), BF16),
            ((orb, rank), F32),
            ((count, rank), F32),
            ((count * cols, rank), F32),
            ((rows, own, rank), F32),
        ],
        [((own * rank // held // 128, orb, 128), F32)] + ([] if held % 16 == 0 else [((orbitals, rank), F32)]),
        6 * orbitals * rank * rank // rows,
    )

    step = width_of(col_width, 256)
    total = []
    for v in range(own):
        core, *total = kernel_call(
            functools.partial(adjoint_kernel, dims, v),
            "adjoint",
            index,
            [*blocks[v], high, low, mine, group, core, *total],
            [((rows, own, rank), F32), ((cols, orb, col_width), F32)],
            [((rows * orb, orbitals), BF16)] * 2 + [((rows * orb, step), F32)] * 2,
            6 * rows * orb * orbitals * rank,
        )

    (factor_part,) = kernel_call(
        functools.partial(factor_kernel, dims),
        "factor",
        index,
        [high, low, mine, every],
        [((orb, col_width), F32)],
        [],
        6 * orbitals * rank * col_width,
    )

    core_gradient = core[0]
    for m in range(1, rows):
        core_gradient = core_gradient + across(core[m], m)
    parts = total[0][0]
    for k in range(1, cols):
        parts = parts + lax.ppermute(total[0][k], "col", [(j, (j + k) % cols) for j in range(cols)])
    factor_gradient = 4.0 * (factor_part - parts)
    return core_gradient, factor_gradient


def solution(mesh):
    placed = (P(("row", "col"), None, None), P(("row", "col"), None), P(("row", "col"), None))
    return jax.shard_map(
        on_device,
        mesh=mesh,
        in_specs=placed,
        out_specs=(P(("row", "col"), None), P("row", "col")),
        check_vma=False,
    )
```

```python
import functools

import jax
import jax.numpy as jnp
from jax import lax
from jax.experimental import pallas as pl
from jax.experimental.pallas import tpu as pltpu
from jax.sharding import PartitionSpec as P

F32 = jnp.float32
BF16 = jnp.bfloat16
VMEM_LIMIT = 32 * 1024 * 1024


def split(a):
    high = a.astype(BF16)
    return high, (a - high.astype(F32)).astype(BF16)


def dot3(a, b):
    both = functools.partial(jnp.dot, preferred_element_type=F32)
    return both(a[0], b[0]) + both(a[0], b[1]) + both(a[1], b[0])


def width_of(extent, most):
    return most if extent % most == 0 else extent


def put_rows(ref, start, values, unit):
    height = values.shape[0]
    if height % unit == 0:
        ref[pl.ds(pl.multiple_of(start, unit), height), :] = values
    else:
        for i in range(height):
            ref[pl.ds(start + i, 1), :] = values[i : i + 1]


def assemble_kernel(dims, places, index_ref, *refs):
    rows, cols, own, held, rank = dims
    pieces = refs[: len(places)]
    high_ref, low_ref, mine_ref, group_ref, all_ref, core_ref, strip_ref, *more = refs[len(places) :]
    r = index_ref[0]
    c = index_ref[1]
    packed = pieces[0].shape[1] - rank
    per_row = rank // packed
    lanes = strip_ref.shape[2]
    orb = cols * held

    seen = 0
    for piece, (mask, first, many) in zip(pieces, places):
        row = lax.bitwise_xor(r, mask)
        for k in range(many):
            line = lax.rem(c + cols - (first + k), cols)
            values = piece[k * held : (k + 1) * held, :rank]
            start = row * orb + line * held
            if more:
                put_rows(more[0], start, values, 8)
            else:
                high, low = split(values)
                put_rows(high_ref, start, high, 16)
                put_rows(low_ref, start, low, 16)
            if mask == 0:
                put_rows(mine_ref, line * held, values, 8)
        taken = many * own
        for h in range(packed // lanes):
            strip_ref[h, : many * held, :] = piece[:, rank + h * lanes : rank + (h + 1) * lanes]
            for j in range(per_row):
                at = j * packed + h * lanes
                all_ref[seen : seen + taken, at : at + lanes] = strip_ref[h, pl.ds(j, taken, stride=per_row), :]
        if first == 0:
            for v in range(own):
                for j in range(per_row):
                    part = piece[pl.ds(v * per_row + j, 1), rank:]
                    group_ref[pl.ds(row * own + v, 1), j * packed : (j + 1) * packed] = part
        seen += taken
    if more:
        high_ref[...], low_ref[...] = split(more[0][...])

    row_width = rank // rows
    block = pl.ds(pl.multiple_of(r * row_width, row_width), row_width)
    left = (high_ref[:, block].T, low_ref[:, block].T)
    weights = split(group_ref[:, block])
    step = width_of(rank, 512)
    for n in range(0, rank, step):
        gram = dot3(left, (high_ref[:, n : n + step], low_ref[:, n : n + step]))
        core = dot3(weights, split(gram * gram))
        for i in range(rows * own):
            core_ref[i // own, i % own : i % own + 1, n : n + step] = core[i : i + 1]


def adjoint_kernel(dims, v, index_ref, *refs):
    rows, cols, own, held, rank = dims
    blocks = 1 if v == 0 else rows // 2 + 1
    vector_refs = refs[:blocks]
    high_ref, low_ref, mine_ref, group_ref, core_ref, *refs = refs[blocks:]
    r = index_ref[0]
    before = refs[0] if v else None
    last = v == own - 1
    *out_refs, sum_ref, left_high, left_low, even_ref, odd_ref = refs[1:] if v else refs
    orb = cols * held
    c = index_ref[1]
    col_width = rank // cols
    step = even_ref.shape[1]
    per_col = col_width // step
    if v == 0:
        left_high[...], left_low[...] = split(vector_refs[0][...])
    else:
        core = pl.multiple_of(lax.rem(r, 2) * orb, orb)
        for i in range(rows):
            values = vector_refs[-1][i // 2 * orb : (i // 2 + 1) * orb] if i % 2 else vector_refs[i // 2][pl.ds(core, orb), :]
            part = slice(i * orb, (i + 1) * orb)
            left_high[part, :], left_low[part, :] = split(values)
    stages = (even_ref, odd_ref)

    def finish(n):
        span = slice(n * step, (n + 1) * step)
        offset = slice((n % per_col) * step, (n % per_col + 1) * step)
        slot = lax.rem(n // per_col + cols - c, cols)
        mine = mine_ref[:, span]
        total = before[slot, :, offset] if v else jnp.zeros_like(mine)
        for i in range(rows):
            adjoint = stages[n % 2][i * orb : (i + 1) * orb, :]
            projection = jnp.sum(adjoint * mine, axis=0, keepdims=True)
            row = i if v == 0 else lax.bitwise_xor(r, i)
            for w in range(own):
                core = core_ref[row, w : w + 1, span]
                core = core - projection if w == v else core
                if last:
                    out_refs[i % 2][i // 2, w : w + 1, span] = core
                else:
                    out_refs[0][row, w : w + 1, span] = core
            total = total + adjoint * group_ref[pl.ds(row * own + v, 1), span]
        sum_ref[slot, :, offset] = total

    for n in range(rank // step):
        span = slice(n * step, (n + 1) * step)
        stages[n % 2][...] = dot3((left_high[...], left_low[...]), (high_ref[:, span], low_ref[:, span]))
        if n:
            finish(n - 1)
    finish(rank // step - 1)


def factor_kernel(dims, index_ref, high_ref, low_ref, mine_ref, all_ref, out_ref):
    rows, cols, own, held, rank = dims
    c = index_ref[1]
    col_width = rank // cols
    block = pl.ds(pl.multiple_of(c * col_width, col_width), col_width)
    left = (high_ref[:, block].T, low_ref[:, block].T)
    weight_left = split(all_ref[:, block].T)
    weight_left = jnp.concatenate([weight_left[0], weight_left[0], weight_left[1]], axis=1)
    mine = jnp.concatenate(split(mine_ref[...].T), axis=1)
    orb = cols * held
    total = jnp.zeros((col_width, 2 * orb), F32)
    side = jnp.zeros((col_width, orb), F32)
    step = width_of(rank, 512)
    for n in range(0, rank, step):
        gram = dot3(left, (high_ref[:, n : n + step], low_ref[:, n : n + step]))
        weight = split(all_ref[:, n : n + step])
        weight = jnp.concatenate([weight[0], weight[1], weight[0]], axis=0)
        mixed = split(gram * jnp.dot(weight_left, weight, preferred_element_type=F32))
        total = total + jnp.dot(mixed[0], mine[n : n + step], preferred_element_type=F32)
        side = side + jnp.dot(mixed[1], mine[n : n + step, :orb], preferred_element_type=F32)
    out_ref[...] = (total[:, :orb] + total[:, orb:] + side).T


def kernel_call(body, name, index, operands, outs, scratch, flops):
    whole = pl.BlockSpec(memory_space=pltpu.VMEM)
    moved = sum(a.size * a.dtype.itemsize for a in operands)
    return pl.pallas_call(
        body,
        out_shape=tuple(pltpu.VMEM(*out) for out in outs),
        in_specs=[pl.BlockSpec(memory_space=pltpu.SMEM)] + [whole] * len(operands),
        out_specs=(whole,) * len(outs),
        scratch_shapes=[pltpu.VMEM(*held) for held in scratch],
        compiler_params=pltpu.CompilerParams(vmem_limit_bytes=VMEM_LIMIT),
        cost_estimate=pl.CostEstimate(flops=flops, bytes_accessed=moved, transcendentals=0),
        name=name,
    )(index, *(pltpu.with_memory_space_constraint(a, pltpu.VMEM) for a in operands))


def on_device(vectors, factor, weights):
    rows = lax.axis_size("row")
    cols = lax.axis_size("col")
    r = lax.axis_index("row")
    c = lax.axis_index("col")
    own, orbitals = vectors.shape[:2]
    held, rank = factor.shape
    orb = orbitals // rows
    col_width = rank // cols
    count = rows * own
    dims = (rows, cols, own, held, rank)
    index = jnp.stack([r, c]).astype(jnp.int32)

    def across(a, mask):
        return lax.ppermute(a, "row", [(i, i ^ mask) for i in range(rows)])

    def spread(vector):
        return lax.all_to_all(vector, "row", split_axis=0, concat_axis=0, tiled=True)

    block = jnp.concatenate([factor, weights.reshape(held, own * rank // held)], axis=1)
    line = [block]
    for k in range(1, cols):
        line.append(lax.ppermute(block, "col", [(j, (j + k) % cols) for j in range(cols)]))
    line[1], vectors = lax.optimization_barrier((line[1], vectors))
    first = spread(vectors[0])
    line, vectors = lax.optimization_barrier((jnp.concatenate(line, axis=0), vectors))

    def pair(v, mask):
        start = ((r ^ mask) // 2) * 2 * orb
        return lax.dynamic_slice(vectors, (v, start, 0), (1, 2 * orb, orbitals))[0]

    later = [[pair(v, mask) for mask in range(0, rows, 2)] for v in range(1, own)]
    whole = [(line, 0, 0, cols)]
    if rows == 8:
        half = cols // 2
        one, two = across(line, 2), across(line, 4)
        give, take, first = lax.optimization_barrier((two[: half * held], one[half * held :], first))
        whole += [(one, 2, 0, cols), (two, 4, 0, cols)]
        whole += [(across(give, 2), 6, 0, half), (across(take, 4), 6, half, cols - half)]
    else:
        whole += [(across(line, m), m, 0, cols) for m in range(2, rows, 2)]
    other = [(across(part, 1), mask + 1, start, many) for part, mask, start, many in whole]
    later, _ = lax.optimization_barrier((later, other[1][0]))
    whole += other
    blocks = [[first]]
    for pairs in later:
        pairs = [pairs[0]] + [across(part, 2 * m) for m, part in enumerate(pairs) if m]
        passed = [lax.dynamic_slice_in_dim(part, (1 - r % 2) * orb, orb, 0) for part in pairs]
        blocks.append(pairs + [across(jnp.concatenate(passed, axis=0), 1)])

    high, low, mine, group, every, core = kernel_call(
        functools.partial(assemble_kernel, dims, [part[1:] for part in whole]),
        "assemble",
        index,
        [part[0] for part in whole],
        [
            ((orbitals, rank), BF16),
            ((orbitals, rank), BF16),
            ((orb, rank), F32),
            ((count, rank), F32),
            ((count * cols, rank), F32),
            ((rows, own, rank), F32),
        ],
        [((own * rank // held // 128, orb, 128), F32)] + ([] if held % 16 == 0 else [((orbitals, rank), F32)]),
        6 * orbitals * rank * rank // rows,
    )

    step = width_of(col_width, 256)
    core, total = [core], None
    for v in range(own):
        shapes = [((rows, own, rank), F32)] if v < own - 1 else [((rows // 2, own, rank), F32)] * 2
        *core, total = kernel_call(
            functools.partial(adjoint_kernel, dims, v),
            "adjoint",
            index,
            [*blocks[v], high, low, mine, group, *core, *([total] if v else [])],
            shapes + [((cols, orb, col_width), F32)],
            [((rows * orb, orbitals), BF16)] * 2 + [((rows * orb, step), F32)] * 2,
            6 * rows * orb * orbitals * rank,
        )

    parts = [total[0]]
    for k in range(1, cols):
        parts.append(lax.ppermute(total[k], "col", [(j, (j + k) % cols) for j in range(cols)]))
    core = core[0] + across(core[1], 1)
    many = rows // 2
    while many > 1:
        many //= 2
        core = core[:many] + across(core[many:], 2 * many)
        if many == 2:
            mine, core = lax.optimization_barrier((mine, core))
    core_gradient = core[0]

    (factor_part,) = kernel_call(
        functools.partial(factor_kernel, dims),
        "factor",
        index,
        [high, low, mine, every],
        [((orb, col_width), F32)],
        [],
        6 * orbitals * rank * col_width,
    )

    factor_gradient = 4.0 * (factor_part - sum(parts[1:], parts[0]))
    return core_gradient, factor_gradient


def solution(mesh):
    placed = (P(("row", "col"), None, None), P(("row", "col"), None), P(("row", "col"), None))
    return jax.shard_map(
        on_device,
        mesh=mesh,
        in_specs=placed,
        out_specs=(P(("row", "col"), None), P("row", "col")),
        check_vma=False,
    )
```

```python
import functools

import jax
import jax.numpy as jnp
from jax import lax
from jax.experimental import pallas as pl
from jax.experimental.pallas import tpu as pltpu
from jax.sharding import PartitionSpec as P

F32 = jnp.float32
BF16 = jnp.bfloat16
VMEM_LIMIT = 32 * 1024 * 1024


def split(a):
    high = a.astype(BF16)
    return high, (a - high.astype(F32)).astype(BF16)


def dot3(a, b):
    both = functools.partial(jnp.dot, preferred_element_type=F32)
    return both(a[0], b[0]) + both(a[0], b[1]) + both(a[1], b[0])


def width_of(extent, most):
    return most if extent % most == 0 else extent


def put_rows(ref, start, values, unit, columns):
    height = values.shape[0]
    if height % unit == 0:
        ref[pl.ds(pl.multiple_of(start, unit), height), columns] = values
    else:
        for i in range(height):
            ref[pl.ds(start + i, 1), columns] = values[i : i + 1]


def assemble_kernel(dims, places, index_ref, *refs):
    rows, cols, own, held, rank = dims
    pieces = refs[: len(places)]
    high_ref, low_ref, mine_ref, group_ref, all_ref, core_ref, strip_ref, *more = refs[len(places) :]
    r = index_ref[0]
    c = index_ref[1]
    packed = pieces[0].shape[1] - rank
    per_row = rank // packed
    lanes = strip_ref.shape[2]
    orb = cols * held
    row_width = rank // rows
    col_width = rank // cols

    def place_of(column):
        return lax.rem(column // col_width + cols - c, cols) * col_width + lax.rem(column, col_width)

    seen = 0
    for piece, (mask, first, many) in zip(pieces, places):
        row = lax.bitwise_xor(r, mask)
        for k in range(many):
            line = lax.rem(c + cols - (first + k), cols)
            start = row * orb + line * held
            for m in range(cols):
                source = pl.ds(pl.multiple_of(lax.rem(c + m, cols) * col_width, col_width), col_width)
                target = slice(m * col_width, (m + 1) * col_width)
                values = piece[k * held : (k + 1) * held, source]
                if more:
                    put_rows(more[0], start, values, 8, target)
                else:
                    high, low = split(values)
                    put_rows(high_ref, start, high, 16, target)
                    put_rows(low_ref, start, low, 16, target)
                if mask == 0:
                    put_rows(mine_ref, line * held, values, 8, target)
        taken = many * own
        for h in range(packed // lanes):
            strip_ref[h, : many * held, :] = piece[:, rank + h * lanes : rank + (h + 1) * lanes]
            for j in range(per_row):
                at = pl.ds(pl.multiple_of(place_of(jnp.int32(j * packed + h * lanes)), lanes), lanes)
                all_ref[seen : seen + taken, at] = strip_ref[h, pl.ds(j, taken, stride=per_row), :]
        if first == 0:
            group_ref[mask * own : (mask + 1) * own, :] = all_ref[seen : seen + own, :]
        seen += taken
    if more:
        high_ref[...], low_ref[...] = split(more[0][...])

    block = pl.ds(pl.multiple_of(place_of(r * row_width), row_width), row_width)
    left = (high_ref[:, block].T, low_ref[:, block].T)
    weights = split(group_ref[:, block])
    step = width_of(rank, 512)
    for n in range(0, rank, step):
        gram = dot3(left, (high_ref[:, n : n + step], low_ref[:, n : n + step]))
        core_ref[:, n : n + step] = dot3(weights, split(gram * gram))


def adjoint_kernel(dims, v, targets, last, index_ref, *refs):
    rows, cols, own, held, rank = dims
    blocks = rows // 2 + 1
    vector_refs = refs[:blocks]
    high_ref, low_ref, mine_ref, group_ref, core_ref, *refs = refs[blocks:]
    before = refs[: len(targets)] if v else None
    refs = refs[len(targets) :] if v else refs
    done_ref, refs = (refs[0], refs[1:]) if last else (None, refs)
    outs = refs[:2] if last else refs[:1]
    sums = refs[len(outs) : len(outs) + len(targets)]
    left_high, left_low, even_ref, odd_ref, rows_ref = refs[len(outs) + len(targets) :]
    r = index_ref[0]
    c = index_ref[1]
    orb = cols * held
    col_width = rank // cols
    step = even_ref.shape[1]
    stages = (even_ref, odd_ref)
    core = pl.multiple_of(lax.rem(r, 2) * orb, orb)
    for i in range(rows):
        values = vector_refs[-1][i // 2 * orb : (i // 2 + 1) * orb] if i % 2 else vector_refs[i // 2][pl.ds(core, orb), :]
        part = slice(i * orb, (i + 1) * orb)
        left_high[part, :], left_low[part, :] = split(values)
    order = [(t, m) for t in range(len(targets)) for m in range(0, col_width, step)]

    def publish(target, values_ref, base):
        at = pl.ds(pl.multiple_of(lax.rem(c + target, cols) * col_width, col_width), col_width)
        for i in range(rows):
            outs[i % 2][i // 2, :, at] = values_ref[i * own : (i + 1) * own, base : base + col_width]

    def finish(n):
        t, m = order[n]
        span = slice(targets[t] * col_width + m, targets[t] * col_width + m + step)
        place = slice(t * col_width + m, t * col_width + m + step)
        kept = rows_ref if last else outs[0]
        kept[:, place] = core_ref[:, span]
        mine = mine_ref[:, span]
        total = before[t][:, m : m + step] if v else jnp.zeros_like(mine)
        for i in range(rows):
            at = i * own + v
            adjoint = stages[n % 2][i * orb : (i + 1) * orb, :]
            projection = jnp.sum(adjoint * mine, axis=0, keepdims=True)
            kept[at : at + 1, place] = core_ref[at : at + 1, span] - projection
            total = total + adjoint * group_ref[at : at + 1, span]
        sums[t][:, m : m + step] = total

    for n, (t, m) in enumerate(order):
        span = slice(targets[t] * col_width + m, targets[t] * col_width + m + step)
        stages[n % 2][...] = dot3((left_high[...], left_low[...]), (high_ref[:, span], low_ref[:, span]))
        if n:
            finish(n - 1)
    finish(len(order) - 1)
    if last:
        others = [k for k in split_targets(cols)[0]]
        for t, target in enumerate(others):
            publish(target, done_ref, t * col_width)
        for t, target in enumerate(targets):
            publish(target, rows_ref, t * col_width)


def split_targets(cols):
    order = list(range(cols // 2, 0, -1)) + list(range(cols // 2 + 1, cols)) + [0]
    return order[: cols // 2], order[cols // 2 :]


def factor_kernel(dims, index_ref, high_ref, low_ref, mine_ref, all_ref, out_ref):
    rows, cols, own, held, rank = dims
    col_width = rank // cols
    block = slice(0, col_width)
    left = (high_ref[:, block].T, low_ref[:, block].T)
    weight_left = split(all_ref[:, block].T)
    weight_left = jnp.concatenate([weight_left[0], weight_left[0], weight_left[1]], axis=1)
    mine = jnp.concatenate(split(mine_ref[...].T), axis=1)
    orb = cols * held
    total = jnp.zeros((col_width, 2 * orb), F32)
    side = jnp.zeros((col_width, orb), F32)
    step = width_of(rank, 512)
    for n in range(0, rank, step):
        gram = dot3(left, (high_ref[:, n : n + step], low_ref[:, n : n + step]))
        weight = split(all_ref[:, n : n + step])
        weight = jnp.concatenate([weight[0], weight[1], weight[0]], axis=0)
        mixed = split(gram * jnp.dot(weight_left, weight, preferred_element_type=F32))
        total = total + jnp.dot(mixed[0], mine[n : n + step], preferred_element_type=F32)
        side = side + jnp.dot(mixed[1], mine[n : n + step, :orb], preferred_element_type=F32)
    out_ref[...] = (total[:, :orb] + total[:, orb:] + side).T


def kernel_call(body, name, index, operands, outs, scratch, flops):
    whole = pl.BlockSpec(memory_space=pltpu.VMEM)
    moved = sum(a.size * a.dtype.itemsize for a in operands)
    return pl.pallas_call(
        body,
        out_shape=tuple(pltpu.VMEM(*out) for out in outs),
        in_specs=[pl.BlockSpec(memory_space=pltpu.SMEM)] + [whole] * len(operands),
        out_specs=(whole,) * len(outs),
        scratch_shapes=[pltpu.VMEM(*held) for held in scratch],
        compiler_params=pltpu.CompilerParams(vmem_limit_bytes=VMEM_LIMIT),
        cost_estimate=pl.CostEstimate(flops=flops, bytes_accessed=moved, transcendentals=0),
        name=name,
    )(index, *(pltpu.with_memory_space_constraint(a, pltpu.VMEM) for a in operands))


def on_device(vectors, factor, weights):
    rows = lax.axis_size("row")
    cols = lax.axis_size("col")
    r = lax.axis_index("row")
    c = lax.axis_index("col")
    own, orbitals = vectors.shape[:2]
    held, rank = factor.shape
    orb = orbitals // rows
    col_width = rank // cols
    count = rows * own
    dims = (rows, cols, own, held, rank)
    index = jnp.stack([r, c]).astype(jnp.int32)

    def across(a, mask):
        return lax.ppermute(a, "row", [(i, i ^ mask) for i in range(rows)])

    def pairs_of(v):
        starts = [((r ^ mask) // 2) * 2 * orb for mask in range(0, rows, 2)]
        return [lax.dynamic_slice(vectors, (v, start, 0), (1, 2 * orb, orbitals))[0] for start in starts]

    def send(pairs):
        return pairs[:1] + [across(pair, 2 * m) for m, pair in enumerate(pairs) if m]

    def complete(pairs):
        passed = [lax.dynamic_slice_in_dim(pair, (1 - r % 2) * orb, orb, 0) for pair in pairs]
        return pairs + [across(jnp.concatenate(passed, axis=0), 1)]

    block = jnp.concatenate([factor, weights.reshape(held, own * rank // held)], axis=1)
    line = [block]
    for k in range(1, cols):
        line.append(lax.ppermute(block, "col", [(j, (j + k) % cols) for j in range(cols)]))
    first = send(pairs_of(0))
    line, first, vectors = lax.optimization_barrier((jnp.concatenate(line, axis=0), first, vectors))

    later = [pairs_of(v) for v in range(1, own)]
    whole = [(line, 0, 0, cols)]
    if rows == 8:
        half = cols // 2
        one, two = across(line, 2), across(line, 4)
        give, take = two[: half * held], one[half * held :]
        whole += [(one, 2, 0, cols), (two, 4, 0, cols)]
        whole += [(across(give, 2), 6, 0, half), (across(take, 4), 6, half, cols - half)]
    else:
        whole += [(across(line, m), m, 0, cols) for m in range(2, rows, 2)]
    other = [(across(part, 1), mask + 1, start, many) for part, mask, start, many in whole]
    whole += other
    later, _ = lax.optimization_barrier((later, other[min(3, len(other) - 1)][0]))
    blocks = [complete(pairs) for pairs in [first] + [send(pairs) for pairs in later]]

    high, low, mine, group, every, core = kernel_call(
        functools.partial(assemble_kernel, dims, [part[1:] for part in whole]),
        "assemble",
        index,
        [part[0] for part in whole],
        [
            ((orbitals, rank), BF16),
            ((orbitals, rank), BF16),
            ((orb, rank), F32),
            ((count, rank), F32),
            ((count * cols, rank), F32),
            ((count, rank), F32),
        ],
        [((own * rank // held // 128, orb, 128), F32)] + ([] if held % 16 == 0 else [((orbitals, rank), F32)]),
        21 * orbitals * rank * rank // rows,
    )

    step = width_of(col_width, 256)

    def adjoint(v, targets, extra, outs, last):
        return kernel_call(
            functools.partial(adjoint_kernel, dims, v, targets, last),
            "adjoint",
            index,
            [*blocks[v], high, low, mine, group, core, *extra],
            outs + [((orb, col_width), F32)] * len(targets),
            [((rows * orb, orbitals), BF16)] * 2
            + [((rows * orb, step), F32)] * 2
            + [((count, len(targets) * col_width if last else 128), F32)],
            9 * rows * orb * orbitals * col_width * len(targets),
        )

    sums = []
    for v in range(own - 1):
        core, *sums = adjoint(v, list(range(cols)), sums, [((count, rank), F32)], False)
    (factor_part,) = kernel_call(
        functools.partial(factor_kernel, dims),
        "factor",
        index,
        [high, low, mine, every],
        [((orb, col_width), F32)],
        [],
        12 * orbitals * rank * col_width,
    )
    blocks[-1], factor_part = lax.optimization_barrier((blocks[-1], factor_part))
    v = own - 1
    early, late = split_targets(cols)
    parts = []
    done, *totals = adjoint(
        v, early, [sums[k] for k in early] if v else [], [((count, len(early) * col_width), F32)], False
    )
    for k, total in zip(early, totals):
        parts.append(lax.ppermute(total, "col", [(j, (j + k) % cols) for j in range(cols)]))
    even, odd, *totals = adjoint(
        v, late, [*([sums[k] for k in late] if v else []), done], [((rows // 2, own, rank), F32)] * 2, True
    )
    for k, total in zip(late, totals):
        parts.append(lax.ppermute(total, "col", [(j, (j + k) % cols) for j in range(cols)]) if k else total)
    core = even + across(odd, 1)
    many = rows // 2
    while many > 1:
        many //= 2
        core = core[:many] + across(core[many:], 2 * many)
    core_gradient = core[0]

    factor_gradient = 4.0 * (factor_part - sum(parts[1:], parts[0]))
    return core_gradient, factor_gradient


def solution(mesh):
    placed = (P(("row", "col"), None, None), P(("row", "col"), None), P(("row", "col"), None))
    return jax.shard_map(
        on_device,
        mesh=mesh,
        in_specs=placed,
        out_specs=(P(("row", "col"), None), P("row", "col")),
        check_vma=False,
    )
```

```python
import functools

import jax
import jax.numpy as jnp
from jax import lax
from jax.experimental import pallas as pl
from jax.experimental.pallas import tpu as pltpu
from jax.sharding import PartitionSpec as P

F32 = jnp.float32
BF16 = jnp.bfloat16
VMEM_LIMIT = 32 * 1024 * 1024


def split(a):
    high = a.astype(BF16)
    return high, (a - high.astype(F32)).astype(BF16)


def dot3(a, b):
    both = functools.partial(jnp.dot, preferred_element_type=F32)
    return both(a[0], b[0]) + both(a[0], b[1]) + both(a[1], b[0])


def width_of(extent, most):
    return most if extent % most == 0 else extent


def put_rows(ref, start, values, unit, columns):
    height = values.shape[0]
    if height % unit == 0:
        ref[pl.ds(pl.multiple_of(start, unit), height), columns] = values
    else:
        for i in range(height):
            ref[pl.ds(start + i, 1), columns] = values[i : i + 1]


def assemble_kernel(dims, places, index_ref, *refs):
    rows, cols, own, held, rank = dims
    pieces = refs[: len(places)]
    high_ref, low_ref, mine_ref, group_ref, all_ref, core_ref, strip_ref, *more = refs[len(places) :]
    r = index_ref[0]
    c = index_ref[1]
    packed = pieces[0].shape[1] - rank
    per_row = rank // packed
    lanes = strip_ref.shape[2]
    orb = cols * held
    row_width = rank // rows
    col_width = rank // cols

    def place_of(column):
        return lax.rem(column // col_width + cols - c, cols) * col_width + lax.rem(column, col_width)

    seen = 0
    for piece, (mask, first, many) in zip(pieces, places):
        row = lax.bitwise_xor(r, mask)
        for k in range(many):
            line = lax.rem(c + cols - (first + k), cols)
            start = row * orb + line * held
            for m in range(cols):
                source = pl.ds(pl.multiple_of(lax.rem(c + m, cols) * col_width, col_width), col_width)
                target = slice(m * col_width, (m + 1) * col_width)
                values = piece[k * held : (k + 1) * held, source]
                if more:
                    put_rows(more[0], start, values, 8, target)
                else:
                    high, low = split(values)
                    put_rows(high_ref, start, high, 16, target)
                    put_rows(low_ref, start, low, 16, target)
                if mask == 0:
                    put_rows(mine_ref, line * held, values, 8, target)
        taken = many * own
        for h in range(packed // lanes):
            strip_ref[h, : many * held, :] = piece[:, rank + h * lanes : rank + (h + 1) * lanes]
            for j in range(per_row):
                at = pl.ds(pl.multiple_of(place_of(jnp.int32(j * packed + h * lanes)), lanes), lanes)
                all_ref[seen : seen + taken, at] = strip_ref[h, pl.ds(j, taken, stride=per_row), :]
        if first == 0:
            group_ref[mask * own : (mask + 1) * own, :] = all_ref[seen : seen + own, :]
        seen += taken
    if more:
        high_ref[...], low_ref[...] = split(more[0][...])

    block = pl.ds(pl.multiple_of(place_of(r * row_width), row_width), row_width)
    left = (high_ref[:, block].T, low_ref[:, block].T)
    weights = split(group_ref[:, block])
    step = width_of(rank, 512)
    for n in range(0, rank, step):
        gram = dot3(left, (high_ref[:, n : n + step], low_ref[:, n : n + step]))
        core_ref[:, n : n + step] = dot3(weights, split(gram * gram))


def adjoint_kernel(dims, v, targets, last, index_ref, *refs):
    rows, cols, own, held, rank = dims
    blocks = rows // 2 + 1
    vector_refs = refs[:blocks]
    high_ref, low_ref, mine_ref, group_ref, core_ref, *refs = refs[blocks:]
    before = refs[: len(targets)] if v else None
    refs = refs[len(targets) :] if v else refs
    done_ref, refs = (refs[0], refs[1:]) if last else (None, refs)
    outs = refs[:2] if last else refs[:1]
    sums = refs[len(outs) : len(outs) + len(targets)]
    left_high, left_low, even_ref, odd_ref, rows_ref = refs[len(outs) + len(targets) :]
    r = index_ref[0]
    c = index_ref[1]
    orb = cols * held
    col_width = rank // cols
    step = even_ref.shape[1]
    stages = (even_ref, odd_ref)
    core = pl.multiple_of(lax.rem(r, 2) * orb, orb)
    for i in range(rows):
        values = vector_refs[-1][i // 2 * orb : (i // 2 + 1) * orb] if i % 2 else vector_refs[i // 2][pl.ds(core, orb), :]
        part = slice(i * orb, (i + 1) * orb)
        left_high[part, :], left_low[part, :] = split(values)
    order = [(t, m) for t in range(len(targets)) for m in range(0, col_width, step)]

    def publish(target, values_ref, base):
        at = pl.ds(pl.multiple_of(lax.rem(c + target, cols) * col_width, col_width), col_width)
        for i in range(rows):
            outs[i % 2][i // 2, :, at] = values_ref[i * own : (i + 1) * own, base : base + col_width]

    def finish(n):
        t, m = order[n]
        span = slice(targets[t] * col_width + m, targets[t] * col_width + m + step)
        place = slice(t * col_width + m, t * col_width + m + step)
        kept = rows_ref if last else outs[0]
        kept[:, place] = core_ref[:, span]
        mine = mine_ref[:, span]
        total = before[t][:, m : m + step] if v else jnp.zeros_like(mine)
        for i in range(rows):
            at = i * own + v
            adjoint = stages[n % 2][i * orb : (i + 1) * orb, :]
            projection = jnp.sum(adjoint * mine, axis=0, keepdims=True)
            kept[at : at + 1, place] = core_ref[at : at + 1, span] - projection
            total = total + adjoint * group_ref[at : at + 1, span]
        sums[t][:, m : m + step] = total

    for n, (t, m) in enumerate(order):
        span = slice(targets[t] * col_width + m, targets[t] * col_width + m + step)
        stages[n % 2][...] = dot3((left_high[...], left_low[...]), (high_ref[:, span], low_ref[:, span]))
        if n:
            finish(n - 1)
    finish(len(order) - 1)
    if last:
        others = [k for k in split_targets(cols)[0]]
        for t, target in enumerate(others):
            publish(target, done_ref, t * col_width)
        for t, target in enumerate(targets):
            publish(target, rows_ref, t * col_width)


def split_targets(cols):
    order = list(range(cols // 2, 0, -1)) + list(range(cols // 2 + 1, cols)) + [0]
    return order[: cols // 2], order[cols // 2 :]


def factor_kernel(dims, index_ref, high_ref, low_ref, mine_ref, all_ref, out_ref):
    rows, cols, own, held, rank = dims
    col_width = rank // cols
    block = slice(0, col_width)
    left = (high_ref[:, block].T, low_ref[:, block].T)
    weight_left = split(all_ref[:, block].T)
    weight_left = jnp.concatenate([weight_left[0], weight_left[0], weight_left[1]], axis=1)
    mine = jnp.concatenate(split(mine_ref[...].T), axis=1)
    orb = cols * held
    total = jnp.zeros((col_width, 2 * orb), F32)
    side = jnp.zeros((col_width, orb), F32)
    step = width_of(rank, 512)
    for n in range(0, rank, step):
        gram = dot3(left, (high_ref[:, n : n + step], low_ref[:, n : n + step]))
        weight = split(all_ref[:, n : n + step])
        weight = jnp.concatenate([weight[0], weight[1], weight[0]], axis=0)
        mixed = split(gram * jnp.dot(weight_left, weight, preferred_element_type=F32))
        total = total + jnp.dot(mixed[0], mine[n : n + step], preferred_element_type=F32)
        side = side + jnp.dot(mixed[1], mine[n : n + step, :orb], preferred_element_type=F32)
    out_ref[...] = (total[:, :orb] + total[:, orb:] + side).T


def kernel_call(body, name, index, operands, outs, scratch, flops):
    whole = pl.BlockSpec(memory_space=pltpu.VMEM)
    moved = sum(a.size * a.dtype.itemsize for a in operands)
    return pl.pallas_call(
        body,
        out_shape=tuple(pltpu.VMEM(*out) for out in outs),
        in_specs=[pl.BlockSpec(memory_space=pltpu.SMEM)] + [whole] * len(operands),
        out_specs=(whole,) * len(outs),
        scratch_shapes=[pltpu.VMEM(*held) for held in scratch],
        compiler_params=pltpu.CompilerParams(vmem_limit_bytes=VMEM_LIMIT),
        cost_estimate=pl.CostEstimate(flops=flops, bytes_accessed=moved, transcendentals=0),
        name=name,
    )(index, *(pltpu.with_memory_space_constraint(a, pltpu.VMEM) for a in operands))


def on_device(vectors, factor, weights):
    rows = lax.axis_size("row")
    cols = lax.axis_size("col")
    r = lax.axis_index("row")
    c = lax.axis_index("col")
    own, orbitals = vectors.shape[:2]
    held, rank = factor.shape
    orb = orbitals // rows
    col_width = rank // cols
    count = rows * own
    dims = (rows, cols, own, held, rank)
    index = jnp.stack([r, c]).astype(jnp.int32)

    def across(a, mask):
        return lax.ppermute(a, "row", [(i, i ^ mask) for i in range(rows)])

    def pairs_of(v):
        starts = [((r ^ mask) // 2) * 2 * orb for mask in range(0, rows, 2)]
        return [lax.dynamic_slice(vectors, (v, start, 0), (1, 2 * orb, orbitals))[0] for start in starts]

    def send(pairs):
        return pairs[:1] + [across(pair, 2 * m) for m, pair in enumerate(pairs) if m]

    def complete(pairs):
        passed = [lax.dynamic_slice_in_dim(pair, (1 - r % 2) * orb, orb, 0) for pair in pairs]
        return pairs + [across(jnp.concatenate(passed, axis=0), 1)]

    block = jnp.concatenate([factor, weights.reshape(held, own * rank // held)], axis=1)
    line = [block]
    for k in range(1, cols):
        line.append(lax.ppermute(block, "col", [(j, (j + k) % cols) for j in range(cols)]))
    first = send(pairs_of(0))
    line, first, vectors = lax.optimization_barrier((jnp.concatenate(line, axis=0), first, vectors))

    later = [pairs_of(v) for v in range(1, own)]
    whole = [(line, 0, 0, cols)]
    if rows == 8:
        half = cols // 2
        one, two = across(line, 2), across(line, 4)
        give, take = two[: half * held], one[half * held :]
        whole += [(one, 2, 0, cols), (two, 4, 0, cols)]
        whole += [(across(give, 2), 6, 0, half), (across(take, 4), 6, half, cols - half)]
    else:
        whole += [(across(line, m), m, 0, cols) for m in range(2, rows, 2)]
    other = [(across(part, 1), mask + 1, start, many) for part, mask, start, many in whole]
    whole += other
    later, _ = lax.optimization_barrier((later, other[min(3, len(other) - 1)][0]))
    sent = [first] + [send(pairs) for pairs in later]

    high, low, mine, group, every, core = kernel_call(
        functools.partial(assemble_kernel, dims, [part[1:] for part in whole]),
        "assemble",
        index,
        [part[0] for part in whole],
        [
            ((orbitals, rank), BF16),
            ((orbitals, rank), BF16),
            ((orb, rank), F32),
            ((count, rank), F32),
            ((count * cols, rank), F32),
            ((count, rank), F32),
        ],
        [((own * rank // held // 128, orb, 128), F32)] + ([] if held % 16 == 0 else [((orbitals, rank), F32)]),
        21 * orbitals * rank * rank // rows,
    )

    step = width_of(col_width, 256)

    def adjoint(v, targets, extra, outs, last):
        return kernel_call(
            functools.partial(adjoint_kernel, dims, v, targets, last),
            "adjoint",
            index,
            [*blocks[v], high, low, mine, group, core, *extra],
            outs + [((orb, col_width), F32)] * len(targets),
            [((rows * orb, orbitals), BF16)] * 2
            + [((rows * orb, step), F32)] * 2
            + [((count, len(targets) * col_width if last else 128), F32)],
            9 * rows * orb * orbitals * col_width * len(targets),
        )

    (factor_part,) = kernel_call(
        functools.partial(factor_kernel, dims),
        "factor",
        index,
        [high, low, mine, every],
        [((orb, col_width), F32)],
        [],
        12 * orbitals * rank * col_width,
    )
    sent[1:], factor_part = lax.optimization_barrier((sent[1:], factor_part))
    blocks = [complete(pairs) for pairs in sent]
    sums = []
    for v in range(own - 1):
        core, *sums = adjoint(v, list(range(cols)), sums, [((count, rank), F32)], False)
    v = own - 1
    early, late = split_targets(cols)
    parts = []
    done, *totals = adjoint(
        v, early, [sums[k] for k in early] if v else [], [((count, len(early) * col_width), F32)], False
    )
    for k, total in zip(early, totals):
        parts.append(lax.ppermute(total, "col", [(j, (j + k) % cols) for j in range(cols)]))
    even, odd, *totals = adjoint(
        v, late, [*([sums[k] for k in late] if v else []), done], [((rows // 2, own, rank), F32)] * 2, True
    )
    for k, total in zip(late, totals):
        parts.append(lax.ppermute(total, "col", [(j, (j + k) % cols) for j in range(cols)]) if k else total)
    core = even + across(odd, 1)
    many = rows // 2
    while many > 1:
        many //= 2
        if many == rows // 4:
            core, parts[: len(early)] = lax.optimization_barrier((core, parts[: len(early)]))
        core = core[:many] + across(core[many:], 2 * many)
    core_gradient = core[0]

    factor_gradient = 4.0 * (factor_part - sum(parts[1:], parts[0]))
    return core_gradient, factor_gradient


def solution(mesh):
    placed = (P(("row", "col"), None, None), P(("row", "col"), None), P(("row", "col"), None))
    return jax.shard_map(
        on_device,
        mesh=mesh,
        in_specs=placed,
        out_specs=(P(("row", "col"), None), P("row", "col")),
        check_vma=False,
    )
```

```python
import functools

import jax
import jax.numpy as jnp
from jax import lax
from jax.experimental import pallas as pl
from jax.experimental.pallas import tpu as pltpu
from jax.sharding import PartitionSpec as P

F32 = jnp.float32
BF16 = jnp.bfloat16
VMEM_LIMIT = 32 * 1024 * 1024


def split(a):
    high = a.astype(BF16)
    return high, (a - high.astype(F32)).astype(BF16)


def dot3(a, b):
    both = functools.partial(jnp.dot, preferred_element_type=F32)
    return both(a[0], b[0]) + both(a[0], b[1]) + both(a[1], b[0])


def width_of(extent, most):
    return most if extent % most == 0 else extent


def put_rows(ref, start, values, unit, columns):
    height = values.shape[0]
    if height % unit == 0:
        ref[pl.ds(pl.multiple_of(start, unit), height), columns] = values
    else:
        for i in range(height):
            ref[pl.ds(start + i, 1), columns] = values[i : i + 1]


def assemble_kernel(dims, places, index_ref, *refs):
    rows, cols, own, held, rank = dims
    pieces = refs[: len(places)]
    high_ref, low_ref, mine_ref, group_ref, all_ref, core_ref, strip_ref, *more = refs[len(places) :]
    r = index_ref[0]
    c = index_ref[1]
    packed = pieces[0].shape[1] - rank
    per_row = rank // packed
    lanes = strip_ref.shape[2]
    orb = cols * held
    row_width = rank // rows
    col_width = rank // cols

    def place_of(column):
        return lax.rem(column // col_width + cols - c, cols) * col_width + lax.rem(column, col_width)

    seen = 0
    for piece, (mask, first, many) in zip(pieces, places):
        row = lax.bitwise_xor(r, mask)
        for k in range(many):
            line = lax.rem(c + cols - (first + k), cols)
            start = row * orb + line * held
            for m in range(cols):
                source = pl.ds(pl.multiple_of(lax.rem(c + m, cols) * col_width, col_width), col_width)
                target = slice(m * col_width, (m + 1) * col_width)
                values = piece[k * held : (k + 1) * held, source]
                if more:
                    put_rows(more[0], start, values, 8, target)
                else:
                    high, low = split(values)
                    put_rows(high_ref, start, high, 16, target)
                    put_rows(low_ref, start, low, 16, target)
                if mask == 0:
                    put_rows(mine_ref, line * held, values, 8, target)
        taken = many * own
        for h in range(packed // lanes):
            strip_ref[h, : many * held, :] = piece[:, rank + h * lanes : rank + (h + 1) * lanes]
            for j in range(per_row):
                at = pl.ds(pl.multiple_of(place_of(jnp.int32(j * packed + h * lanes)), lanes), lanes)
                all_ref[seen : seen + taken, at] = strip_ref[h, pl.ds(j, taken, stride=per_row), :]
        if first == 0:
            group_ref[mask * own : (mask + 1) * own, :] = all_ref[seen : seen + own, :]
        seen += taken
    if more:
        high_ref[...], low_ref[...] = split(more[0][...])

    block = pl.ds(pl.multiple_of(place_of(r * row_width), row_width), row_width)
    left = (high_ref[:, block].T, low_ref[:, block].T)
    weights = split(group_ref[:, block])
    step = width_of(rank, 512)
    for n in range(0, rank, step):
        gram = dot3(left, (high_ref[:, n : n + step], low_ref[:, n : n + step]))
        core_ref[:, n : n + step] = dot3(weights, split(gram * gram))


def adjoint_kernel(dims, v, targets, last, index_ref, *refs):
    rows, cols, own, held, rank = dims
    blocks = rows // 2 + 1
    vector_refs = refs[:blocks]
    high_ref, low_ref, mine_ref, group_ref, core_ref, *refs = refs[blocks:]
    before = refs[: len(targets)] if v else None
    refs = refs[len(targets) :] if v else refs
    outs = refs[:2] if last else refs[:1]
    sums = refs[len(outs) : len(outs) + len(targets)]
    left_high, left_low, even_ref, odd_ref, rows_ref = refs[len(outs) + len(targets) :]
    r = index_ref[0]
    c = index_ref[1]
    orb = cols * held
    col_width = rank // cols
    step = even_ref.shape[1]
    stages = (even_ref, odd_ref)
    core = pl.multiple_of(lax.rem(r, 2) * orb, orb)
    for i in range(rows):
        values = vector_refs[-1][i // 2 * orb : (i // 2 + 1) * orb] if i % 2 else vector_refs[i // 2][pl.ds(core, orb), :]
        part = slice(i * orb, (i + 1) * orb)
        left_high[part, :], left_low[part, :] = split(values)
    order = [(t, m) for t in range(len(targets)) for m in range(0, col_width, step)]

    def publish(target, values_ref, base):
        at = pl.ds(pl.multiple_of(lax.rem(c + target, cols) * col_width, col_width), col_width)
        for i in range(rows):
            outs[i % 2][i // 2, :, at] = values_ref[i * own : (i + 1) * own, base : base + col_width]

    def finish(n):
        t, m = order[n]
        span = slice(targets[t] * col_width + m, targets[t] * col_width + m + step)
        place = slice(t * col_width + m, t * col_width + m + step)
        kept = rows_ref if last else outs[0]
        kept[:, place] = core_ref[:, span]
        mine = mine_ref[:, span]
        total = before[t][:, m : m + step] if v else jnp.zeros_like(mine)
        for i in range(rows):
            at = i * own + v
            adjoint = stages[n % 2][i * orb : (i + 1) * orb, :]
            projection = jnp.sum(adjoint * mine, axis=0, keepdims=True)
            kept[at : at + 1, place] = core_ref[at : at + 1, span] - projection
            total = total + adjoint * group_ref[at : at + 1, span]
        sums[t][:, m : m + step] = total

    for n, (t, m) in enumerate(order):
        span = slice(targets[t] * col_width + m, targets[t] * col_width + m + step)
        stages[n % 2][...] = dot3((left_high[...], left_low[...]), (high_ref[:, span], low_ref[:, span]))
        if n:
            finish(n - 1)
    finish(len(order) - 1)
    if last:
        for t, target in enumerate(targets):
            publish(target, rows_ref, t * col_width)


def factor_kernel(dims, index_ref, high_ref, low_ref, mine_ref, all_ref, out_ref):
    rows, cols, own, held, rank = dims
    col_width = rank // cols
    block = slice(0, col_width)
    left = (high_ref[:, block].T, low_ref[:, block].T)
    weight_left = split(all_ref[:, block].T)
    weight_left = jnp.concatenate([weight_left[0], weight_left[0], weight_left[1]], axis=1)
    mine = jnp.concatenate(split(mine_ref[...].T), axis=1)
    orb = cols * held
    total = jnp.zeros((col_width, 2 * orb), F32)
    side = jnp.zeros((col_width, orb), F32)
    step = width_of(rank, 512)
    for n in range(0, rank, step):
        gram = dot3(left, (high_ref[:, n : n + step], low_ref[:, n : n + step]))
        weight = split(all_ref[:, n : n + step])
        weight = jnp.concatenate([weight[0], weight[1], weight[0]], axis=0)
        mixed = split(gram * jnp.dot(weight_left, weight, preferred_element_type=F32))
        total = total + jnp.dot(mixed[0], mine[n : n + step], preferred_element_type=F32)
        side = side + jnp.dot(mixed[1], mine[n : n + step, :orb], preferred_element_type=F32)
    out_ref[...] = (total[:, :orb] + total[:, orb:] + side).T


def kernel_call(body, name, index, operands, outs, scratch, flops):
    whole = pl.BlockSpec(memory_space=pltpu.VMEM)
    moved = sum(a.size * a.dtype.itemsize for a in operands)
    return pl.pallas_call(
        body,
        out_shape=tuple(pltpu.VMEM(*out) for out in outs),
        in_specs=[pl.BlockSpec(memory_space=pltpu.SMEM)] + [whole] * len(operands),
        out_specs=(whole,) * len(outs),
        scratch_shapes=[pltpu.VMEM(*held) for held in scratch],
        compiler_params=pltpu.CompilerParams(vmem_limit_bytes=VMEM_LIMIT),
        cost_estimate=pl.CostEstimate(flops=flops, bytes_accessed=moved, transcendentals=0),
        name=name,
    )(index, *(pltpu.with_memory_space_constraint(a, pltpu.VMEM) for a in operands))


def on_device(vectors, factor, weights):
    rows = lax.axis_size("row")
    cols = lax.axis_size("col")
    r = lax.axis_index("row")
    c = lax.axis_index("col")
    own, orbitals = vectors.shape[:2]
    held, rank = factor.shape
    orb = orbitals // rows
    col_width = rank // cols
    count = rows * own
    dims = (rows, cols, own, held, rank)
    index = jnp.stack([r, c]).astype(jnp.int32)

    def across(a, mask):
        return lax.ppermute(a, "row", [(i, i ^ mask) for i in range(rows)])

    def pairs_of(v):
        starts = [((r ^ mask) // 2) * 2 * orb for mask in range(0, rows, 2)]
        return [lax.dynamic_slice(vectors, (v, start, 0), (1, 2 * orb, orbitals))[0] for start in starts]

    def send(pairs):
        return pairs[:1] + [across(pair, 2 * m) for m, pair in enumerate(pairs) if m]

    def complete(pairs):
        passed = [lax.dynamic_slice_in_dim(pair, (1 - r % 2) * orb, orb, 0) for pair in pairs]
        return pairs + [across(jnp.concatenate(passed, axis=0), 1)]

    block = jnp.concatenate([factor, weights.reshape(held, own * rank // held)], axis=1)
    line = [block]
    for k in range(1, cols):
        line.append(lax.ppermute(block, "col", [(j, (j + k) % cols) for j in range(cols)]))
    first = send(pairs_of(0))
    line, first, vectors = lax.optimization_barrier((jnp.concatenate(line, axis=0), first, vectors))

    later = [pairs_of(v) for v in range(1, own)]
    whole = [(line, 0, 0, cols)]
    other = [across(line, 1)]
    if rows == 8:
        half = cols // 2
        one, two = across(line, 2), across(line, 4)
        give, take, later = lax.optimization_barrier((two[: half * held], one[half * held :], later))
        whole += [(one, 2, 0, cols), (two, 4, 0, cols)]
        other += [across(one, 1), across(two, 1)]
        whole += [(across(give, 2), 6, 0, half), (across(take, 4), 6, half, cols - half)]
    else:
        whole += [(across(line, m), m, 0, cols) for m in range(2, rows, 2)]
    later, other = lax.optimization_barrier((later, other))
    other += [across(part[0], 1) for part in whole[len(other) :]]
    whole += [(part, mask + 1, start, many) for part, (_, mask, start, many) in zip(other, whole)]
    sent = [first] + [send(pairs) for pairs in later]
    high, low, mine, group, every, core = kernel_call(
        functools.partial(assemble_kernel, dims, [part[1:] for part in whole]),
        "assemble",
        index,
        [part[0] for part in whole],
        [
            ((orbitals, rank), BF16),
            ((orbitals, rank), BF16),
            ((orb, rank), F32),
            ((count, rank), F32),
            ((count * cols, rank), F32),
            ((count, rank), F32),
        ],
        [((own * rank // held // 128, orb, 128), F32)] + ([] if held % 16 == 0 else [((orbitals, rank), F32)]),
        21 * orbitals * rank * rank // rows,
    )

    step = width_of(col_width, 256)

    def adjoint(v, targets, extra, outs, last):
        return kernel_call(
            functools.partial(adjoint_kernel, dims, v, targets, last),
            "adjoint",
            index,
            [*blocks[v], high, low, mine, group, core, *extra],
            outs + [((orb, col_width), F32)] * len(targets),
            [((rows * orb, orbitals), BF16)] * 2
            + [((rows * orb, step), F32)] * 2
            + [((count, len(targets) * col_width if last else 128), F32)],
            9 * rows * orb * orbitals * col_width * len(targets),
        )

    sent[1:], core = lax.optimization_barrier((sent[1:], core))
    blocks = [complete(pairs) for pairs in sent]
    sums = []
    for v in range(own - 1):
        core, *sums = adjoint(v, list(range(cols)), sums, [((count, rank), F32)], False)
    even, odd, *sums = adjoint(own - 1, list(range(cols)), sums, [((rows // 2, own, rank), F32)] * 2, True)
    parts = sums[:1]
    for k in range(1, cols):
        parts.append(lax.ppermute(sums[k], "col", [(j, (j + k) % cols) for j in range(cols)]))
    core = even + across(odd, 1)
    many = rows // 2
    while many > 1:
        many //= 2
        if many == rows // 4:
            mine, core = lax.optimization_barrier((mine, core))
        core = core[:many] + across(core[many:], 2 * many)
    core_gradient = core[0]

    (factor_part,) = kernel_call(
        functools.partial(factor_kernel, dims),
        "factor",
        index,
        [high, low, mine, every],
        [((orb, col_width), F32)],
        [],
        12 * orbitals * rank * col_width,
    )
    factor_gradient = 4.0 * (factor_part - sum(parts[1:], parts[0]))
    return core_gradient, factor_gradient


def solution(mesh):
    placed = (P(("row", "col"), None, None), P(("row", "col"), None), P(("row", "col"), None))
    return jax.shard_map(
        on_device,
        mesh=mesh,
        in_specs=placed,
        out_specs=(P(("row", "col"), None), P("row", "col")),
        check_vma=False,
    )
```

```python
import functools

import jax
import jax.numpy as jnp
from jax import lax
from jax.experimental import pallas as pl
from jax.experimental.pallas import tpu as pltpu
from jax.sharding import PartitionSpec as P

F32 = jnp.float32
BF16 = jnp.bfloat16
VMEM_LIMIT = 32 * 1024 * 1024


def split(a):
    high = a.astype(BF16)
    return high, (a - high.astype(F32)).astype(BF16)


def dot3(a, b):
    both = functools.partial(jnp.dot, preferred_element_type=F32)
    return both(a[0], b[0]) + both(a[0], b[1]) + both(a[1], b[0])


def width_of(extent, most):
    return most if extent % most == 0 else extent


def put_rows(ref, start, values, unit, columns):
    height = values.shape[0]
    if height % unit == 0:
        ref[pl.ds(pl.multiple_of(start, unit), height), columns] = values
    else:
        for i in range(height):
            ref[pl.ds(start + i, 1), columns] = values[i : i + 1]


def assemble_kernel(dims, places, index_ref, *refs):
    rows, cols, own, held, rank = dims
    count = 1 + max(place[0] for place in places)
    pieces = refs[:count]
    high_ref, low_ref, mine_ref, group_ref, all_ref, core_ref, strip_ref, *more = refs[count:]
    r = index_ref[0]
    c = index_ref[1]
    packed = pieces[0].shape[1] - rank
    per_row = rank // packed
    lanes = strip_ref.shape[2]
    orb = cols * held
    row_width = rank // rows
    col_width = rank // cols

    def place_of(column):
        return lax.rem(column // col_width + cols - c, cols) * col_width + lax.rem(column, col_width)

    seen = 0
    for part, base, mask, first, many in places:
        piece = pieces[part]
        row = lax.bitwise_xor(r, mask)
        for k in range(many):
            line = lax.rem(c + cols - (first + k), cols)
            start = row * orb + line * held
            for m in range(cols):
                source = pl.ds(pl.multiple_of(lax.rem(c + m, cols) * col_width, col_width), col_width)
                target = slice(m * col_width, (m + 1) * col_width)
                values = piece[base + k * held : base + (k + 1) * held, source]
                if more:
                    put_rows(more[0], start, values, 8, target)
                else:
                    high, low = split(values)
                    put_rows(high_ref, start, high, 16, target)
                    put_rows(low_ref, start, low, 16, target)
                if mask == 0:
                    put_rows(mine_ref, line * held, values, 8, target)
        taken = many * own
        for h in range(packed // lanes):
            strip_ref[h, : many * held, :] = piece[base : base + many * held, rank + h * lanes : rank + (h + 1) * lanes]
            for j in range(per_row):
                at = pl.ds(pl.multiple_of(place_of(jnp.int32(j * packed + h * lanes)), lanes), lanes)
                all_ref[seen : seen + taken, at] = strip_ref[h, pl.ds(j, taken, stride=per_row), :]
        if first == 0:
            group_ref[mask * own : (mask + 1) * own, :] = all_ref[seen : seen + own, :]
        seen += taken
    if more:
        high_ref[...], low_ref[...] = split(more[0][...])

    block = pl.ds(pl.multiple_of(place_of(r * row_width), row_width), row_width)
    left = (high_ref[:, block].T, low_ref[:, block].T)
    weights = split(group_ref[:, block])
    step = width_of(rank, 512)
    for n in range(0, rank, step):
        gram = dot3(left, (high_ref[:, n : n + step], low_ref[:, n : n + step]))
        core_ref[:, n : n + step] = dot3(weights, split(gram * gram))


def adjoint_kernel(dims, v, targets, last, index_ref, *refs):
    rows, cols, own, held, rank = dims
    blocks = rows // 2 + 1
    vector_refs = refs[:blocks]
    high_ref, low_ref, mine_ref, group_ref, core_ref, *refs = refs[blocks:]
    before = refs[: len(targets)] if v else None
    refs = refs[len(targets) :] if v else refs
    outs = refs[:2] if last else refs[:1]
    sums = refs[len(outs) : len(outs) + len(targets)]
    left_high, left_low, even_ref, odd_ref, rows_ref = refs[len(outs) + len(targets) :]
    r = index_ref[0]
    c = index_ref[1]
    orb = cols * held
    col_width = rank // cols
    step = even_ref.shape[1]
    stages = (even_ref, odd_ref)
    core = pl.multiple_of(lax.rem(r, 2) * orb, orb)
    for i in range(rows):
        values = vector_refs[-1][i // 2 * orb : (i // 2 + 1) * orb] if i % 2 else vector_refs[i // 2][pl.ds(core, orb), :]
        part = slice(i * orb, (i + 1) * orb)
        left_high[part, :], left_low[part, :] = split(values)
    order = [(t, m) for t in range(len(targets)) for m in range(0, col_width, step)]

    def publish(target, values_ref, base):
        at = pl.ds(pl.multiple_of(lax.rem(c + target, cols) * col_width, col_width), col_width)
        for i in range(rows):
            outs[i % 2][i // 2, :, at] = values_ref[i * own : (i + 1) * own, base : base + col_width]

    def finish(n):
        t, m = order[n]
        span = slice(targets[t] * col_width + m, targets[t] * col_width + m + step)
        place = slice(t * col_width + m, t * col_width + m + step)
        kept = rows_ref if last else outs[0]
        kept[:, place] = core_ref[:, span]
        mine = mine_ref[:, span]
        total = before[t][:, m : m + step] if v else jnp.zeros_like(mine)
        for i in range(rows):
            at = i * own + v
            adjoint = stages[n % 2][i * orb : (i + 1) * orb, :]
            projection = jnp.sum(adjoint * mine, axis=0, keepdims=True)
            kept[at : at + 1, place] = core_ref[at : at + 1, span] - projection
            total = total + adjoint * group_ref[at : at + 1, span]
        sums[t][:, m : m + step] = total

    for n, (t, m) in enumerate(order):
        span = slice(targets[t] * col_width + m, targets[t] * col_width + m + step)
        stages[n % 2][...] = dot3((left_high[...], left_low[...]), (high_ref[:, span], low_ref[:, span]))
        if n:
            finish(n - 1)
    finish(len(order) - 1)
    if last:
        for t, target in enumerate(targets):
            publish(target, rows_ref, t * col_width)


def factor_kernel(dims, index_ref, high_ref, low_ref, mine_ref, all_ref, out_ref):
    rows, cols, own, held, rank = dims
    col_width = rank // cols
    block = slice(0, col_width)
    left = (high_ref[:, block].T, low_ref[:, block].T)
    weight_left = split(all_ref[:, block].T)
    weight_left = jnp.concatenate([weight_left[0], weight_left[0], weight_left[1]], axis=1)
    mine = jnp.concatenate(split(mine_ref[...].T), axis=1)
    orb = cols * held
    total = jnp.zeros((col_width, 2 * orb), F32)
    side = jnp.zeros((col_width, orb), F32)
    step = width_of(rank, 512)
    for n in range(0, rank, step):
        gram = dot3(left, (high_ref[:, n : n + step], low_ref[:, n : n + step]))
        weight = split(all_ref[:, n : n + step])
        weight = jnp.concatenate([weight[0], weight[1], weight[0]], axis=0)
        mixed = split(gram * jnp.dot(weight_left, weight, preferred_element_type=F32))
        total = total + jnp.dot(mixed[0], mine[n : n + step], preferred_element_type=F32)
        side = side + jnp.dot(mixed[1], mine[n : n + step, :orb], preferred_element_type=F32)
    out_ref[...] = (total[:, :orb] + total[:, orb:] + side).T


def kernel_call(body, name, index, operands, outs, scratch, flops):
    whole = pl.BlockSpec(memory_space=pltpu.VMEM)
    moved = sum(a.size * a.dtype.itemsize for a in operands)
    return pl.pallas_call(
        body,
        out_shape=tuple(pltpu.VMEM(*out) for out in outs),
        in_specs=[pl.BlockSpec(memory_space=pltpu.SMEM)] + [whole] * len(operands),
        out_specs=(whole,) * len(outs),
        scratch_shapes=[pltpu.VMEM(*held) for held in scratch],
        compiler_params=pltpu.CompilerParams(vmem_limit_bytes=VMEM_LIMIT),
        cost_estimate=pl.CostEstimate(flops=flops, bytes_accessed=moved, transcendentals=0),
        name=name,
    )(index, *(pltpu.with_memory_space_constraint(a, pltpu.VMEM) for a in operands))


def on_device(vectors, factor, weights):
    rows = lax.axis_size("row")
    cols = lax.axis_size("col")
    r = lax.axis_index("row")
    c = lax.axis_index("col")
    own, orbitals = vectors.shape[:2]
    held, rank = factor.shape
    orb = orbitals // rows
    col_width = rank // cols
    count = rows * own
    dims = (rows, cols, own, held, rank)
    index = jnp.stack([r, c]).astype(jnp.int32)

    def across(a, mask):
        return lax.ppermute(a, "row", [(i, i ^ mask) for i in range(rows)])

    def pairs_of(v):
        starts = [((r ^ mask) // 2) * 2 * orb for mask in range(0, rows, 2)]
        return [lax.dynamic_slice(vectors, (v, start, 0), (1, 2 * orb, orbitals))[0] for start in starts]

    def send(pairs):
        return pairs[:1] + [across(pair, 2 * m) for m, pair in enumerate(pairs) if m]

    def complete(pairs):
        passed = [lax.dynamic_slice_in_dim(pair, (1 - r % 2) * orb, orb, 0) for pair in pairs]
        return pairs + [across(jnp.concatenate(passed, axis=0), 1)]

    block = jnp.concatenate([factor, weights.reshape(held, own * rank // held)], axis=1)
    line = [block]
    for k in range(1, cols):
        line.append(lax.ppermute(block, "col", [(j, (j + k) % cols) for j in range(cols)]))
    first = send(pairs_of(0))
    line, first, vectors = lax.optimization_barrier((jnp.concatenate(line, axis=0), first, vectors))

    later = [pairs_of(v) for v in range(1, own)]
    pieces, masks = [line], [0]
    if rows == 8:
        half = cols // 2
        one, two = across(line, 2), across(line, 4)
        give, take, later = lax.optimization_barrier((two[: half * held], one[half * held :], later))
        pieces += [jnp.concatenate([one, two], axis=0), jnp.concatenate([across(give, 2), across(take, 4)], axis=0)]
        masks += [2, 4, 6]
    else:
        masks += list(range(2, rows, 2))
        pieces += [across(line, m) for m in masks[1:]]
    sent = [first] + [send(pairs) for pairs in later]
    pieces += [across(piece, 1) for piece in pieces]
    places = []
    for part, piece in enumerate(pieces):
        for base in range(0, piece.shape[0], orb):
            mask = masks[len(places)] if len(places) < len(masks) else masks[len(places) - len(masks)] + 1
            places.append((part, base, mask, 0, cols))

    high, low, mine, group, every, core = kernel_call(
        functools.partial(assemble_kernel, dims, places),
        "assemble",
        index,
        pieces,
        [
            ((orbitals, rank), BF16),
            ((orbitals, rank), BF16),
            ((orb, rank), F32),
            ((count, rank), F32),
            ((count * cols, rank), F32),
            ((count, rank), F32),
        ],
        [((own * rank // held // 128, orb, 128), F32)] + ([] if held % 16 == 0 else [((orbitals, rank), F32)]),
        1 * orbitals * rank * rank // rows,
    )

    step = width_of(col_width, 256)

    def adjoint(v, targets, extra, outs, last):
        return kernel_call(
            functools.partial(adjoint_kernel, dims, v, targets, last),
            "adjoint",
            index,
            [*blocks[v], high, low, mine, group, core, *extra],
            outs + [((orb, col_width), F32)] * len(targets),
            [((rows * orb, orbitals), BF16)] * 2
            + [((rows * orb, step), F32)] * 2
            + [((count, len(targets) * col_width if last else 128), F32)],
            9 * rows * orb * orbitals * col_width * len(targets),
        )

    sent[1:], core = lax.optimization_barrier((sent[1:], core))
    blocks = [complete(pairs) for pairs in sent]
    sums = []
    for v in range(own - 1):
        core, *sums = adjoint(v, list(range(cols)), sums, [((count, rank), F32)], False)
    even, odd, *sums = adjoint(own - 1, list(range(cols)), sums, [((rows // 2, own, rank), F32)] * 2, True)
    parts = sums[:1]
    for k in range(1, cols):
        parts.append(lax.ppermute(sums[k], "col", [(j, (j + k) % cols) for j in range(cols)]))
    core = even + across(odd, 1)
    many = rows // 2
    while many > 1:
        many //= 2
        if many == rows // 4:
            mine, core = lax.optimization_barrier((mine, core))
        core = core[:many] + across(core[many:], 2 * many)
    core_gradient = core[0]

    (factor_part,) = kernel_call(
        functools.partial(factor_kernel, dims),
        "factor",
        index,
        [high, low, mine, every],
        [((orb, col_width), F32)],
        [],
        12 * orbitals * rank * col_width,
    )
    factor_gradient = 4.0 * (factor_part - sum(parts[1:], parts[0]))
    return core_gradient, factor_gradient


def solution(mesh):
    placed = (P(("row", "col"), None, None), P(("row", "col"), None), P(("row", "col"), None))
    return jax.shard_map(
        on_device,
        mesh=mesh,
        in_specs=placed,
        out_specs=(P(("row", "col"), None), P("row", "col")),
        check_vma=False,
    )
```

```python
import functools

import jax
import jax.numpy as jnp
from jax import lax
from jax.experimental import pallas as pl
from jax.experimental.pallas import tpu as pltpu
from jax.sharding import PartitionSpec as P

F32 = jnp.float32
BF16 = jnp.bfloat16
VMEM_LIMIT = 32 * 1024 * 1024


def split(a):
    high = a.astype(BF16)
    return high, (a - high.astype(F32)).astype(BF16)


def dot3(a, b):
    both = functools.partial(jnp.dot, preferred_element_type=F32)
    return both(a[0], b[0]) + both(a[0], b[1]) + both(a[1], b[0])


def dot_stacked(left, rows_ref, span):
    both = functools.partial(jnp.dot, preferred_element_type=F32)
    return both(left[0], rows_ref[:, span]) + both(left[1], rows_ref[: rows_ref.shape[0] // 2, span])


def transposed_left(rows_ref, columns):
    orbitals = rows_ref.shape[0] // 2
    high = rows_ref[:orbitals, columns].T
    return jnp.concatenate([high, high], axis=1), rows_ref[orbitals:, columns].T


def width_of(extent, most):
    return most if extent % most == 0 else extent


def put_rows(ref, start, values, unit, columns):
    height = values.shape[0]
    if height % unit == 0:
        ref[pl.ds(pl.multiple_of(start, unit), height), columns] = values
    else:
        for i in range(height):
            ref[pl.ds(start + i, 1), columns] = values[i : i + 1]


def assemble_kernel(dims, places, index_ref, *refs):
    rows, cols, own, held, rank = dims
    pieces = refs[: len(places)]
    rows_ref, mine_ref, group_ref, all_ref, core_ref, strip_ref, *more = refs[len(places) :]
    orbitals = rows * cols * held
    r = index_ref[0]
    c = index_ref[1]
    packed = pieces[0].shape[1] - rank
    per_row = rank // packed
    lanes = strip_ref.shape[2]
    orb = cols * held
    row_width = rank // rows
    col_width = rank // cols

    def place_of(column):
        return lax.rem(column // col_width + cols - c, cols) * col_width + lax.rem(column, col_width)

    seen = 0
    for piece, (mask, first, many) in zip(pieces, places):
        row = lax.bitwise_xor(r, mask)
        for k in range(many):
            line = lax.rem(c + cols - (first + k), cols)
            start = row * orb + line * held
            for m in range(cols):
                source = pl.ds(pl.multiple_of(lax.rem(c + m, cols) * col_width, col_width), col_width)
                target = slice(m * col_width, (m + 1) * col_width)
                values = piece[k * held : (k + 1) * held, source]
                if more:
                    put_rows(more[0], start, values, 8, target)
                else:
                    high, low = split(values)
                    put_rows(rows_ref, start, high, 16, target)
                    put_rows(rows_ref, orbitals + start, low, 16, target)
                if mask == 0:
                    put_rows(mine_ref, line * held, values, 8, target)
        taken = many * own
        for h in range(packed // lanes):
            strip_ref[h, : many * held, :] = piece[:, rank + h * lanes : rank + (h + 1) * lanes]
            for j in range(per_row):
                at = pl.ds(pl.multiple_of(place_of(jnp.int32(j * packed + h * lanes)), lanes), lanes)
                all_ref[seen : seen + taken, at] = strip_ref[h, pl.ds(j, taken, stride=per_row), :]
        if first == 0:
            group_ref[mask * own : (mask + 1) * own, :] = all_ref[seen : seen + own, :]
        seen += taken
    if more:
        rows_ref[:orbitals, :], rows_ref[orbitals:, :] = split(more[0][...])

    block = pl.ds(pl.multiple_of(place_of(r * row_width), row_width), row_width)
    left = transposed_left(rows_ref, block)
    weights = split(group_ref[:, block])
    step = width_of(rank, 512)
    for n in range(0, rank, step):
        gram = dot_stacked(left, rows_ref, slice(n, n + step))
        core_ref[:, n : n + step] = dot3(weights, split(gram * gram))


def adjoint_kernel(dims, v, targets, last, index_ref, *refs):
    rows, cols, own, held, rank = dims
    blocks = rows // 2 + (1 if v < own - 1 else rows // 2)
    vector_refs = refs[:blocks]
    rows_in_ref, mine_ref, group_ref, core_ref, *refs = refs[blocks:]
    before = refs[: len(targets)] if v else None
    refs = refs[len(targets) :] if v else refs
    outs = refs[:2] if last else refs[:1]
    sums = refs[len(outs) : len(outs) + len(targets)]
    left_high, left_low, even_ref, odd_ref, rows_ref = refs[len(outs) + len(targets) :]
    r = index_ref[0]
    c = index_ref[1]
    orb = cols * held
    col_width = rank // cols
    step = even_ref.shape[1]
    stages = (even_ref, odd_ref)
    core = pl.multiple_of(lax.rem(r, 2) * orb, orb)
    for i in range(rows):
        if i % 2 == 0:
            values = vector_refs[i // 2][pl.ds(core, orb), :]
        elif v < own - 1:
            values = vector_refs[-1][i // 2 * orb : (i // 2 + 1) * orb]
        else:
            values = vector_refs[rows // 2 + i // 2][...]
        part = slice(i * orb, (i + 1) * orb)
        high, low = split(values)
        left_high[part, :], left_low[part, :] = jnp.concatenate([high, high], axis=1), low
    order = [(t, m) for t in range(len(targets)) for m in range(0, col_width, step)]

    def publish(target, values_ref, base):
        at = pl.ds(pl.multiple_of(lax.rem(c + target, cols) * col_width, col_width), col_width)
        for i in range(rows):
            outs[i % 2][i // 2, :, at] = values_ref[i * own : (i + 1) * own, base : base + col_width]

    def finish(n):
        t, m = order[n]
        span = slice(targets[t] * col_width + m, targets[t] * col_width + m + step)
        place = slice(t * col_width + m, t * col_width + m + step)
        kept = rows_ref if last else outs[0]
        kept[:, place] = core_ref[:, span]
        mine = mine_ref[:, span]
        total = before[t][:, m : m + step] if v else jnp.zeros_like(mine)
        for i in range(rows):
            at = i * own + v
            adjoint = stages[n % 2][i * orb : (i + 1) * orb, :]
            projection = jnp.sum(adjoint * mine, axis=0, keepdims=True)
            kept[at : at + 1, place] = core_ref[at : at + 1, span] - projection
            total = total + adjoint * group_ref[at : at + 1, span]
        sums[t][:, m : m + step] = total

    for n, (t, m) in enumerate(order):
        span = slice(targets[t] * col_width + m, targets[t] * col_width + m + step)
        stages[n % 2][...] = dot_stacked((left_high[...], left_low[...]), rows_in_ref, span)
        if n:
            finish(n - 1)
    finish(len(order) - 1)
    if last:
        for t, target in enumerate(targets):
            publish(target, rows_ref, t * col_width)


def factor_kernel(dims, index_ref, rows_ref, mine_ref, all_ref, out_ref):
    rows, cols, own, held, rank = dims
    col_width = rank // cols
    block = slice(0, col_width)
    left = transposed_left(rows_ref, block)
    weight_left = split(all_ref[:, block].T)
    weight_left = jnp.concatenate([weight_left[0], weight_left[0], weight_left[1]], axis=1)
    mine = jnp.concatenate(split(mine_ref[...].T), axis=1)
    orb = cols * held
    total = jnp.zeros((col_width, 2 * orb), F32)
    side = jnp.zeros((col_width, orb), F32)
    step = width_of(rank, 512)
    for n in range(0, rank, step):
        gram = dot_stacked(left, rows_ref, slice(n, n + step))
        weight = split(all_ref[:, n : n + step])
        weight = jnp.concatenate([weight[0], weight[1], weight[0]], axis=0)
        mixed = split(gram * jnp.dot(weight_left, weight, preferred_element_type=F32))
        total = total + jnp.dot(mixed[0], mine[n : n + step], preferred_element_type=F32)
        side = side + jnp.dot(mixed[1], mine[n : n + step, :orb], preferred_element_type=F32)
    out_ref[...] = (total[:, :orb] + total[:, orb:] + side).T


def kernel_call(body, name, index, operands, outs, scratch, flops):
    whole = pl.BlockSpec(memory_space=pltpu.VMEM)
    moved = sum(a.size * a.dtype.itemsize for a in operands)
    return pl.pallas_call(
        body,
        out_shape=tuple(pltpu.VMEM(*out) for out in outs),
        in_specs=[pl.BlockSpec(memory_space=pltpu.SMEM)] + [whole] * len(operands),
        out_specs=(whole,) * len(outs),
        scratch_shapes=[pltpu.VMEM(*held) for held in scratch],
        compiler_params=pltpu.CompilerParams(vmem_limit_bytes=VMEM_LIMIT),
        cost_estimate=pl.CostEstimate(flops=flops, bytes_accessed=moved, transcendentals=0),
        name=name,
    )(index, *(pltpu.with_memory_space_constraint(a, pltpu.VMEM) for a in operands))


def on_device(vectors, factor, weights):
    rows = lax.axis_size("row")
    cols = lax.axis_size("col")
    r = lax.axis_index("row")
    c = lax.axis_index("col")
    own, orbitals = vectors.shape[:2]
    held, rank = factor.shape
    orb = orbitals // rows
    col_width = rank // cols
    count = rows * own
    dims = (rows, cols, own, held, rank)
    index = jnp.stack([r, c]).astype(jnp.int32)

    def across(a, mask):
        return lax.ppermute(a, "row", [(i, i ^ mask) for i in range(rows)])

    def pairs_of(v):
        starts = [((r ^ mask) // 2) * 2 * orb for mask in range(0, rows, 2)]
        return [lax.dynamic_slice(vectors, (v, start, 0), (1, 2 * orb, orbitals))[0] for start in starts]

    def send(pairs):
        return pairs[:1] + [across(pair, 2 * m) for m, pair in enumerate(pairs) if m]

    def complete(pairs, together):
        passed = [lax.dynamic_slice_in_dim(pair, (1 - r % 2) * orb, orb, 0) for pair in pairs]
        return pairs + [across(part, 1) for part in ([jnp.concatenate(passed, axis=0)] if together else passed)]

    block = jnp.concatenate([factor, weights.reshape(held, own * rank // held)], axis=1)
    line = [block]
    for k in range(1, cols):
        line.append(lax.ppermute(block, "col", [(j, (j + k) % cols) for j in range(cols)]))
    first = send(pairs_of(0))
    line, first, vectors = lax.optimization_barrier((jnp.concatenate(line, axis=0), first, vectors))

    later = [pairs_of(v) for v in range(1, own)]
    whole = [(line, 0, 0, cols)]
    other = [across(line, 1)]
    if rows == 8:
        half = cols // 2
        one, two = across(line, 2), across(line, 4)
        give, take, later = lax.optimization_barrier((two[: half * held], one[half * held :], later))
        give, take = across(give, 2), across(take, 4)
        one, two, give = lax.optimization_barrier((one, two, give))
        whole += [(one, 2, 0, cols), (two, 4, 0, cols), (give, 6, 0, half), (take, 6, half, cols - half)]
    else:
        whole += [(across(line, m), m, 0, cols) for m in range(2, rows, 2)]
    other += [across(part[0], 1) for part in whole[len(other) :]]
    whole += [(part, mask + 1, start, many) for part, (_, mask, start, many) in zip(other, whole)]
    sent = [first] + [send(pairs) for pairs in later]
    stacked, mine, group, every, core = kernel_call(
        functools.partial(assemble_kernel, dims, [part[1:] for part in whole]),
        "assemble",
        index,
        [part[0] for part in whole],
        [
            ((2 * orbitals, rank), BF16),
            ((orb, rank), F32),
            ((count, rank), F32),
            ((count * cols, rank), F32),
            ((count, rank), F32),
        ],
        [((own * rank // held // 128, orb, 128), F32)] + ([] if held % 16 == 0 else [((orbitals, rank), F32)]),
        21 * orbitals * rank * rank // rows,
    )

    step = width_of(col_width, 256)

    def adjoint(v, targets, extra, outs, last):
        return kernel_call(
            functools.partial(adjoint_kernel, dims, v, targets, last),
            "adjoint",
            index,
            [*blocks[v], stacked, mine, group, core, *extra],
            outs + [((orb, col_width), F32)] * len(targets),
            [((rows * orb, 2 * orbitals), BF16), ((rows * orb, orbitals), BF16)]
            + [((rows * orb, step), F32)] * 2
            + [((count, len(targets) * col_width if last else 128), F32)],
            9 * rows * orb * orbitals * col_width * len(targets),
        )

    blocks = [complete(pairs, True) for pairs in sent[:-1]]
    sums = []
    for v in range(own - 1):
        core, *sums = adjoint(v, list(range(cols)), sums, [((count, rank), F32)], False)
    sent[-1][1:], core = lax.optimization_barrier((sent[-1][1:], core))
    blocks.append(complete(sent[-1], False))
    even, odd, *sums = adjoint(own - 1, list(range(cols)), sums, [((rows // 2, own, rank), F32)] * 2, True)
    parts = sums[:1]
    for k in range(1, cols):
        parts.append(lax.ppermute(sums[k], "col", [(j, (j + k) % cols) for j in range(cols)]))
    core = even + across(odd, 1)
    many = rows // 2
    while many > 1:
        many //= 2
        if many == rows // 4:
            mine, core = lax.optimization_barrier((mine, core))
        core = core[:many] + across(core[many:], 2 * many)
    core_gradient = core[0]

    (factor_part,) = kernel_call(
        functools.partial(factor_kernel, dims),
        "factor",
        index,
        [stacked, mine, every],
        [((orb, col_width), F32)],
        [],
        12 * orbitals * rank * col_width,
    )
    factor_gradient = 4.0 * (factor_part - sum(parts[1:], parts[0]))
    return core_gradient, factor_gradient


def solution(mesh):
    placed = (P(("row", "col"), None, None), P(("row", "col"), None), P(("row", "col"), None))
    return jax.shard_map(
        on_device,
        mesh=mesh,
        in_specs=placed,
        out_specs=(P(("row", "col"), None), P("row", "col")),
        check_vma=False,
    )
```

```python
import functools

import jax
import jax.numpy as jnp
from jax import lax
from jax.experimental import pallas as pl
from jax.experimental.pallas import tpu as pltpu
from jax.sharding import PartitionSpec as P

F32 = jnp.float32
BF16 = jnp.bfloat16
VMEM_LIMIT = 32 * 1024 * 1024


def split(a):
    high = a.astype(BF16)
    return high, (a - high.astype(F32)).astype(BF16)


def dot3(a, b):
    both = functools.partial(jnp.dot, preferred_element_type=F32)
    return both(a[0], b[0]) + both(a[0], b[1]) + both(a[1], b[0])


def dot_stacked(left, rows_ref, span):
    both = functools.partial(jnp.dot, preferred_element_type=F32)
    return both(left[0], rows_ref[:, span]) + both(left[1], rows_ref[: rows_ref.shape[0] // 2, span])


def transposed_left(rows_ref, columns):
    orbitals = rows_ref.shape[0] // 2
    high = rows_ref[:orbitals, columns].T
    return jnp.concatenate([high, high], axis=1), rows_ref[orbitals:, columns].T


def width_of(extent, most):
    return most if extent % most == 0 else extent


def put_rows(ref, start, values, unit, columns):
    height = values.shape[0]
    if height % unit == 0:
        ref[pl.ds(pl.multiple_of(start, unit), height), columns] = values
    else:
        for i in range(height):
            ref[pl.ds(start + i, 1), columns] = values[i : i + 1]


def assemble_kernel(dims, places, index_ref, *refs):
    rows, cols, own, held, rank = dims
    pieces = refs[: len(places)]
    rows_ref, mine_ref, group_ref, all_ref, core_ref, strip_ref, *more = refs[len(places) :]
    orbitals = rows * cols * held
    r = index_ref[0]
    c = index_ref[1]
    packed = pieces[0].shape[1] - rank
    per_row = rank // packed
    lanes = strip_ref.shape[2]
    orb = cols * held
    row_width = rank // rows
    col_width = rank // cols

    def place_of(column):
        return lax.rem(column // col_width + cols - c, cols) * col_width + lax.rem(column, col_width)

    seen = 0
    for piece, (mask, first, many) in zip(pieces, places):
        row = lax.bitwise_xor(r, mask)
        for k in range(many):
            line = lax.rem(c + cols - (first + k), cols)
            start = row * orb + line * held
            for m in range(cols):
                source = pl.ds(pl.multiple_of(lax.rem(c + m, cols) * col_width, col_width), col_width)
                target = slice(m * col_width, (m + 1) * col_width)
                values = piece[k * held : (k + 1) * held, source]
                if more:
                    put_rows(more[0], start, values, 8, target)
                else:
                    high, low = split(values)
                    put_rows(rows_ref, start, high, 16, target)
                    put_rows(rows_ref, orbitals + start, low, 16, target)
                if mask == 0:
                    put_rows(mine_ref, line * held, values, 8, target)
        taken = many * own
        for h in range(packed // lanes):
            strip_ref[h, : many * held, :] = piece[:, rank + h * lanes : rank + (h + 1) * lanes]
            for j in range(per_row):
                at = pl.ds(pl.multiple_of(place_of(jnp.int32(j * packed + h * lanes)), lanes), lanes)
                all_ref[seen : seen + taken, at] = strip_ref[h, pl.ds(j, taken, stride=per_row), :]
        if first == 0:
            group_ref[mask * own : (mask + 1) * own, :] = all_ref[seen : seen + own, :]
        seen += taken
    if more:
        rows_ref[:orbitals, :], rows_ref[orbitals:, :] = split(more[0][...])

    block = pl.ds(pl.multiple_of(place_of(r * row_width), row_width), row_width)
    left = transposed_left(rows_ref, block)
    weights = split(group_ref[:, block])
    step = width_of(rank, 512)
    for n in range(0, rank, step):
        gram = dot_stacked(left, rows_ref, slice(n, n + step))
        core_ref[:, n : n + step] = dot3(weights, split(gram * gram))


def adjoint_kernel(dims, v, targets, last, index_ref, *refs):
    rows, cols, own, held, rank = dims
    blocks = rows // 2 + (1 if v < own - 1 else rows // 2)
    vector_refs = refs[:blocks]
    rows_in_ref, mine_ref, group_ref, core_ref, *refs = refs[blocks:]
    before = refs[: len(targets)] if v else None
    refs = refs[len(targets) :] if v else refs
    outs = refs[:2] if last else refs[:1]
    sums = refs[len(outs) : len(outs) + len(targets)]
    left_high, left_low, even_ref, odd_ref, rows_ref = refs[len(outs) + len(targets) :]
    r = index_ref[0]
    c = index_ref[1]
    orb = cols * held
    col_width = rank // cols
    step = even_ref.shape[1]
    stages = (even_ref, odd_ref)
    core = pl.multiple_of(lax.rem(r, 2) * orb, orb)
    for i in range(rows):
        if i % 2 == 0:
            values = vector_refs[i // 2][pl.ds(core, orb), :]
        elif v < own - 1:
            values = vector_refs[-1][i // 2 * orb : (i // 2 + 1) * orb]
        else:
            values = vector_refs[rows // 2 + i // 2][...]
        part = slice(i * orb, (i + 1) * orb)
        high, low = split(values)
        left_high[part, :], left_low[part, :] = jnp.concatenate([high, high], axis=1), low
    order = [(t, m) for t in range(len(targets)) for m in range(0, col_width, step)]

    def publish(target, values_ref, base):
        at = pl.ds(pl.multiple_of(lax.rem(c + target, cols) * col_width, col_width), col_width)
        for i in range(rows):
            outs[i % 2][i // 2, :, at] = values_ref[i * own : (i + 1) * own, base : base + col_width]

    def finish(n):
        t, m = order[n]
        span = slice(targets[t] * col_width + m, targets[t] * col_width + m + step)
        place = slice(t * col_width + m, t * col_width + m + step)
        kept = rows_ref if last else outs[0]
        kept[:, place] = core_ref[:, span]
        mine = mine_ref[:, span]
        total = before[t][:, m : m + step] if v else jnp.zeros_like(mine)
        for i in range(rows):
            at = i * own + v
            adjoint = stages[n % 2][i * orb : (i + 1) * orb, :]
            projection = jnp.sum(adjoint * mine, axis=0, keepdims=True)
            kept[at : at + 1, place] = core_ref[at : at + 1, span] - projection
            total = total + adjoint * group_ref[at : at + 1, span]
        sums[t][:, m : m + step] = total

    for n, (t, m) in enumerate(order):
        span = slice(targets[t] * col_width + m, targets[t] * col_width + m + step)
        stages[n % 2][...] = dot_stacked((left_high[...], left_low[...]), rows_in_ref, span)
        if n:
            finish(n - 1)
    finish(len(order) - 1)
    if last:
        for t, target in enumerate(targets):
            publish(target, rows_ref, t * col_width)


def factor_kernel(dims, index_ref, rows_ref, mine_ref, all_ref, out_ref):
    rows, cols, own, held, rank = dims
    col_width = rank // cols
    block = slice(0, col_width)
    left = transposed_left(rows_ref, block)
    weight_left = split(all_ref[:, block].T)
    weight_left = jnp.concatenate([weight_left[0], weight_left[0], weight_left[1]], axis=1)
    mine = jnp.concatenate(split(mine_ref[...].T), axis=1)
    orb = cols * held
    total = jnp.zeros((col_width, 2 * orb), F32)
    side = jnp.zeros((col_width, orb), F32)
    step = width_of(rank, 512)
    for n in range(0, rank, step):
        gram = dot_stacked(left, rows_ref, slice(n, n + step))
        weight = split(all_ref[:, n : n + step])
        weight = jnp.concatenate([weight[0], weight[1], weight[0]], axis=0)
        mixed = split(gram * jnp.dot(weight_left, weight, preferred_element_type=F32))
        total = total + jnp.dot(mixed[0], mine[n : n + step], preferred_element_type=F32)
        side = side + jnp.dot(mixed[1], mine[n : n + step, :orb], preferred_element_type=F32)
    out_ref[...] = (total[:, :orb] + total[:, orb:] + side).T


def kernel_call(body, name, index, operands, outs, scratch, flops):
    whole = pl.BlockSpec(memory_space=pltpu.VMEM)
    moved = sum(a.size * a.dtype.itemsize for a in operands)
    return pl.pallas_call(
        body,
        out_shape=tuple(pltpu.VMEM(*out) for out in outs),
        in_specs=[pl.BlockSpec(memory_space=pltpu.SMEM)] + [whole] * len(operands),
        out_specs=(whole,) * len(outs),
        scratch_shapes=[pltpu.VMEM(*held) for held in scratch],
        compiler_params=pltpu.CompilerParams(vmem_limit_bytes=VMEM_LIMIT),
        cost_estimate=pl.CostEstimate(flops=flops, bytes_accessed=moved, transcendentals=0),
        name=name,
    )(index, *(pltpu.with_memory_space_constraint(a, pltpu.VMEM) for a in operands))


def on_device(vectors, factor, weights):
    rows = lax.axis_size("row")
    cols = lax.axis_size("col")
    r = lax.axis_index("row")
    c = lax.axis_index("col")
    own, orbitals = vectors.shape[:2]
    held, rank = factor.shape
    orb = orbitals // rows
    col_width = rank // cols
    count = rows * own
    dims = (rows, cols, own, held, rank)
    index = jnp.stack([r, c]).astype(jnp.int32)

    def across(a, mask):
        return lax.ppermute(a, "row", [(i, i ^ mask) for i in range(rows)])

    def pairs_of(v):
        starts = [((r ^ mask) // 2) * 2 * orb for mask in range(0, rows, 2)]
        return [lax.dynamic_slice(vectors, (v, start, 0), (1, 2 * orb, orbitals))[0] for start in starts]

    def send(pairs):
        return pairs[:1] + [across(pair, 2 * m) for m, pair in enumerate(pairs) if m]

    def complete(pairs, together):
        passed = [lax.dynamic_slice_in_dim(pair, (1 - r % 2) * orb, orb, 0) for pair in pairs]
        return pairs + [across(part, 1) for part in ([jnp.concatenate(passed, axis=0)] if together else passed)]

    block = jnp.concatenate([factor, weights.reshape(held, own * rank // held)], axis=1)
    line = [block]
    for k in range(1, cols):
        line.append(lax.ppermute(block, "col", [(j, (j + k) % cols) for j in range(cols)]))
    first = send(pairs_of(0))
    line, first, vectors = lax.optimization_barrier((jnp.concatenate(line, axis=0), first, vectors))

    later = [pairs_of(v) for v in range(1, own)]
    whole = [(line, 0, 0, cols)]
    other = [across(line, 1)]
    if rows == 8:
        half = cols // 2
        one, two = across(line, 2), across(line, 4)
        give, take, later = lax.optimization_barrier((two[: half * held], one[half * held :], later))
        give, take = across(give, 2), across(take, 4)
        sent = [send(pairs) for pairs in later]
        one, two, give = lax.optimization_barrier((one, two, give))
        take, sent[-1][1:3] = lax.optimization_barrier((take, sent[-1][1:3]))
        whole += [(one, 2, 0, cols), (two, 4, 0, cols), (give, 6, 0, half), (take, 6, half, cols - half)]
    else:
        whole += [(across(line, m), m, 0, cols) for m in range(2, rows, 2)]
        sent = [send(pairs) for pairs in later]
    other += [across(part[0], 1) for part in whole[len(other) :]]
    whole += [(part, mask + 1, start, many) for part, (_, mask, start, many) in zip(other, whole)]
    sent = [first] + sent
    stacked, mine, group, every, core = kernel_call(
        functools.partial(assemble_kernel, dims, [part[1:] for part in whole]),
        "assemble",
        index,
        [part[0] for part in whole],
        [
            ((2 * orbitals, rank), BF16),
            ((orb, rank), F32),
            ((count, rank), F32),
            ((count * cols, rank), F32),
            ((count, rank), F32),
        ],
        [((own * rank // held // 128, orb, 128), F32)] + ([] if held % 16 == 0 else [((orbitals, rank), F32)]),
        21 * orbitals * rank * rank // rows,
    )

    step = width_of(col_width, 256)

    def adjoint(v, targets, extra, outs, last):
        return kernel_call(
            functools.partial(adjoint_kernel, dims, v, targets, last),
            "adjoint",
            index,
            [*blocks[v], stacked, mine, group, core, *extra],
            outs + [((orb, col_width), F32)] * len(targets),
            [((rows * orb, 2 * orbitals), BF16), ((rows * orb, orbitals), BF16)]
            + [((rows * orb, step), F32)] * 2
            + [((count, len(targets) * col_width if last else 128), F32)],
            9 * rows * orb * orbitals * col_width * len(targets),
        )

    blocks = [complete(pairs, True) for pairs in sent[:-1]]
    sums = []
    for v in range(own - 1):
        core, *sums = adjoint(v, list(range(cols)), sums, [((count, rank), F32)], False)
    sent[-1][1:], core = lax.optimization_barrier((sent[-1][1:], core))
    blocks.append(complete(sent[-1], False))
    even, odd, *sums = adjoint(own - 1, list(range(cols)), sums, [((rows // 2, own, rank), F32)] * 2, True)
    parts = sums[:1]
    for k in range(1, cols):
        parts.append(lax.ppermute(sums[k], "col", [(j, (j + k) % cols) for j in range(cols)]))
    core = even + across(odd, 1)
    many = rows // 2
    while many > 1:
        many //= 2
        if many == rows // 4:
            mine, core = lax.optimization_barrier((mine, core))
        core = core[:many] + across(core[many:], 2 * many)
    core_gradient = core[0]

    (factor_part,) = kernel_call(
        functools.partial(factor_kernel, dims),
        "factor",
        index,
        [stacked, mine, every],
        [((orb, col_width), F32)],
        [],
        12 * orbitals * rank * col_width,
    )
    factor_gradient = 4.0 * (factor_part - sum(parts[1:], parts[0]))
    return core_gradient, factor_gradient


def solution(mesh):
    placed = (P(("row", "col"), None, None), P(("row", "col"), None), P(("row", "col"), None))
    return jax.shard_map(
        on_device,
        mesh=mesh,
        in_specs=placed,
        out_specs=(P(("row", "col"), None), P("row", "col")),
        check_vma=False,
    )
```

```python
import functools

import jax
import jax.numpy as jnp
from jax import lax
from jax.experimental import pallas as pl
from jax.experimental.pallas import tpu as pltpu
from jax.sharding import PartitionSpec as P

F32 = jnp.float32
BF16 = jnp.bfloat16
VMEM_LIMIT = 32 * 1024 * 1024


def split(a):
    high = a.astype(BF16)
    return high, (a - high.astype(F32)).astype(BF16)


def dot3(a, b):
    both = functools.partial(jnp.dot, preferred_element_type=F32)
    return both(a[0], b[0]) + both(a[0], b[1]) + both(a[1], b[0])


def dot_stacked(left, rows_ref, span):
    both = functools.partial(jnp.dot, preferred_element_type=F32)
    return both(left[0], rows_ref[:, span]) + both(left[1], rows_ref[: rows_ref.shape[0] // 2, span])


def transposed_left(rows_ref, columns):
    orbitals = rows_ref.shape[0] // 2
    high = rows_ref[:orbitals, columns].T
    return jnp.concatenate([high, high], axis=1), rows_ref[orbitals:, columns].T


def width_of(extent, most):
    return most if extent % most == 0 else extent


def put_rows(ref, start, values, unit, columns):
    height = values.shape[0]
    if height % unit == 0:
        ref[pl.ds(pl.multiple_of(start, unit), height), columns] = values
    else:
        for i in range(height):
            ref[pl.ds(start + i, 1), columns] = values[i : i + 1]


def assemble_kernel(dims, places, index_ref, *refs):
    rows, cols, own, held, rank = dims
    pieces = refs[: len(places)]
    rows_ref, mine_ref, group_ref, all_ref, core_ref, strip_ref, *more = refs[len(places) :]
    orbitals = rows * cols * held
    r = index_ref[0]
    c = index_ref[1]
    packed = pieces[0].shape[1] - rank
    per_row = rank // packed
    lanes = strip_ref.shape[2]
    orb = cols * held
    row_width = rank // rows
    col_width = rank // cols

    def place_of(column):
        return lax.rem(column // col_width + cols - c, cols) * col_width + lax.rem(column, col_width)

    seen = 0
    for piece, (mask, first, many) in zip(pieces, places):
        row = lax.bitwise_xor(r, mask)
        for k in range(many):
            line = lax.rem(c + cols - (first + k), cols)
            start = row * orb + line * held
            for m in range(cols):
                source = pl.ds(pl.multiple_of(lax.rem(c + m, cols) * col_width, col_width), col_width)
                target = slice(m * col_width, (m + 1) * col_width)
                values = piece[k * held : (k + 1) * held, source]
                if more:
                    put_rows(more[0], start, values, 8, target)
                else:
                    high, low = split(values)
                    put_rows(rows_ref, start, high, 16, target)
                    put_rows(rows_ref, orbitals + start, low, 16, target)
                if mask == 0:
                    put_rows(mine_ref, line * held, values, 8, target)
        taken = many * own
        for h in range(packed // lanes):
            strip_ref[h, : many * held, :] = piece[:, rank + h * lanes : rank + (h + 1) * lanes]
            for j in range(per_row):
                at = pl.ds(pl.multiple_of(place_of(jnp.int32(j * packed + h * lanes)), lanes), lanes)
                all_ref[seen : seen + taken, at] = strip_ref[h, pl.ds(j, taken, stride=per_row), :]
        if first == 0:
            group_ref[mask * own : (mask + 1) * own, :] = all_ref[seen : seen + own, :]
        seen += taken
    if more:
        rows_ref[:orbitals, :], rows_ref[orbitals:, :] = split(more[0][...])

    block = pl.ds(pl.multiple_of(place_of(r * row_width), row_width), row_width)
    left = transposed_left(rows_ref, block)
    weights = split(group_ref[:, block])
    step = width_of(rank, 512)
    for n in range(0, rank, step):
        gram = dot_stacked(left, rows_ref, slice(n, n + step))
        core_ref[:, n : n + step] = dot3(weights, split(gram * gram))


def adjoint_kernel(dims, v, targets, last, index_ref, *refs):
    rows, cols, own, held, rank = dims
    blocks = rows // 2 + (1 if v < own - 1 else rows // 2)
    vector_refs = refs[:blocks]
    rows_in_ref, mine_ref, group_ref, core_ref, *refs = refs[blocks:]
    before = refs[: len(targets)] if v else None
    refs = refs[len(targets) :] if v else refs
    outs = refs[:2] if last else refs[:1]
    sums = refs[len(outs) : len(outs) + len(targets)]
    left_high, left_low, even_ref, odd_ref, rows_ref = refs[len(outs) + len(targets) :]
    r = index_ref[0]
    c = index_ref[1]
    orb = cols * held
    col_width = rank // cols
    step = even_ref.shape[1]
    stages = (even_ref, odd_ref)
    core = pl.multiple_of(lax.rem(r, 2) * orb, orb)
    for i in range(rows):
        if i % 2 == 0:
            values = vector_refs[i // 2][pl.ds(core, orb), :]
        elif v < own - 1:
            values = vector_refs[-1][i // 2 * orb : (i // 2 + 1) * orb]
        else:
            values = vector_refs[rows // 2 + i // 2][...]
        part = slice(i * orb, (i + 1) * orb)
        high, low = split(values)
        left_high[part, :], left_low[part, :] = jnp.concatenate([high, high], axis=1), low
    order = [(t, m) for t in range(len(targets)) for m in range(0, col_width, step)]

    def publish(target, values_ref, base):
        at = pl.ds(pl.multiple_of(lax.rem(c + target, cols) * col_width, col_width), col_width)
        for i in range(rows):
            outs[i % 2][i // 2, :, at] = values_ref[i * own : (i + 1) * own, base : base + col_width]

    def finish(n):
        t, m = order[n]
        span = slice(targets[t] * col_width + m, targets[t] * col_width + m + step)
        place = slice(t * col_width + m, t * col_width + m + step)
        kept = rows_ref if last else outs[0]
        kept[:, place] = core_ref[:, span]
        mine = mine_ref[:, span]
        total = before[t][:, m : m + step] if v else jnp.zeros_like(mine)
        for i in range(rows):
            at = i * own + v
            adjoint = stages[n % 2][i * orb : (i + 1) * orb, :]
            projection = jnp.sum(adjoint * mine, axis=0, keepdims=True)
            kept[at : at + 1, place] = core_ref[at : at + 1, span] - projection
            total = total + adjoint * group_ref[at : at + 1, span]
        sums[t][:, m : m + step] = total

    for n, (t, m) in enumerate(order):
        span = slice(targets[t] * col_width + m, targets[t] * col_width + m + step)
        stages[n % 2][...] = dot_stacked((left_high[...], left_low[...]), rows_in_ref, span)
        if n:
            finish(n - 1)
    finish(len(order) - 1)
    if last:
        for t, target in enumerate(targets):
            publish(target, rows_ref, t * col_width)


def factor_kernel(dims, index_ref, rows_ref, mine_ref, all_ref, out_ref):
    rows, cols, own, held, rank = dims
    col_width = rank // cols
    block = slice(0, col_width)
    left = transposed_left(rows_ref, block)
    weight_left = split(all_ref[:, block].T)
    weight_left = jnp.concatenate([weight_left[0], weight_left[0], weight_left[1]], axis=1)
    mine = jnp.concatenate(split(mine_ref[...].T), axis=1)
    orb = cols * held
    total = jnp.zeros((col_width, 2 * orb), F32)
    side = jnp.zeros((col_width, orb), F32)
    step = width_of(rank, 512)
    for n in range(0, rank, step):
        gram = dot_stacked(left, rows_ref, slice(n, n + step))
        weight = split(all_ref[:, n : n + step])
        weight = jnp.concatenate([weight[0], weight[1], weight[0]], axis=0)
        mixed = split(gram * jnp.dot(weight_left, weight, preferred_element_type=F32))
        total = total + jnp.dot(mixed[0], mine[n : n + step], preferred_element_type=F32)
        side = side + jnp.dot(mixed[1], mine[n : n + step, :orb], preferred_element_type=F32)
    out_ref[...] = (total[:, :orb] + total[:, orb:] + side).T


def kernel_call(body, name, index, operands, outs, scratch, flops):
    whole = pl.BlockSpec(memory_space=pltpu.VMEM)
    moved = sum(a.size * a.dtype.itemsize for a in operands)
    return pl.pallas_call(
        body,
        out_shape=tuple(pltpu.VMEM(*out) for out in outs),
        in_specs=[pl.BlockSpec(memory_space=pltpu.SMEM)] + [whole] * len(operands),
        out_specs=(whole,) * len(outs),
        scratch_shapes=[pltpu.VMEM(*held) for held in scratch],
        compiler_params=pltpu.CompilerParams(vmem_limit_bytes=VMEM_LIMIT),
        cost_estimate=pl.CostEstimate(flops=flops, bytes_accessed=moved, transcendentals=0),
        name=name,
    )(index, *(pltpu.with_memory_space_constraint(a, pltpu.VMEM) for a in operands))


def on_device(vectors, factor, weights):
    rows = lax.axis_size("row")
    cols = lax.axis_size("col")
    r = lax.axis_index("row")
    c = lax.axis_index("col")
    own, orbitals = vectors.shape[:2]
    held, rank = factor.shape
    orb = orbitals // rows
    col_width = rank // cols
    count = rows * own
    dims = (rows, cols, own, held, rank)
    index = jnp.stack([r, c]).astype(jnp.int32)

    def across(a, mask):
        return lax.ppermute(a, "row", [(i, i ^ mask) for i in range(rows)])

    def pairs_of(v):
        starts = [((r ^ mask) // 2) * 2 * orb for mask in range(0, rows, 2)]
        return [lax.dynamic_slice(vectors, (v, start, 0), (1, 2 * orb, orbitals))[0] for start in starts]

    def send(pairs):
        return pairs[:1] + [across(pair, 2 * m) for m, pair in enumerate(pairs) if m]

    def complete(pairs, together):
        passed = [lax.dynamic_slice_in_dim(pair, (1 - r % 2) * orb, orb, 0) for pair in pairs]
        return pairs + [across(part, 1) for part in ([jnp.concatenate(passed, axis=0)] if together else passed)]

    block = jnp.concatenate([factor, weights.reshape(held, own * rank // held)], axis=1)
    line = [block]
    for k in range(1, cols):
        line.append(lax.ppermute(block, "col", [(j, (j + k) % cols) for j in range(cols)]))
    first = send(pairs_of(0))
    line, first, vectors = lax.optimization_barrier((jnp.concatenate(line, axis=0), first, vectors))

    later = [pairs_of(v) for v in range(1, own)]
    whole = [(line, 0, 0, cols)]
    other = [across(line, 1)]
    if rows == 8:
        half = cols // 2
        one, two = across(line, 2), across(line, 4)
        give, take, later = lax.optimization_barrier((two[: half * held], one[half * held :], later))
        whole += [(one, 2, 0, cols), (two, 4, 0, cols)]
        other += [across(one, 1), across(two, 1)]
        whole += [(across(give, 2), 6, 0, half), (across(take, 4), 6, half, cols - half)]
    else:
        whole += [(across(line, m), m, 0, cols) for m in range(2, rows, 2)]
    later, other[0] = lax.optimization_barrier((later, other[0]))
    other += [across(part[0], 1) for part in whole[len(other) :]]
    whole += [(part, mask + 1, start, many) for part, (_, mask, start, many) in zip(other, whole)]
    sent = [first] + [send(pairs) for pairs in later]
    stacked, mine, group, every, core = kernel_call(
        functools.partial(assemble_kernel, dims, [part[1:] for part in whole]),
        "assemble",
        index,
        [part[0] for part in whole],
        [
            ((2 * orbitals, rank), BF16),
            ((orb, rank), F32),
            ((count, rank), F32),
            ((count * cols, rank), F32),
            ((count, rank), F32),
        ],
        [((own * rank // held // 128, orb, 128), F32)] + ([] if held % 16 == 0 else [((orbitals, rank), F32)]),
        21 * orbitals * rank * rank // rows,
    )

    step = width_of(col_width, 256)

    def adjoint(v, targets, extra, outs, last):
        return kernel_call(
            functools.partial(adjoint_kernel, dims, v, targets, last),
            "adjoint",
            index,
            [*blocks[v], stacked, mine, group, core, *extra],
            outs + [((orb, col_width), F32)] * len(targets),
            [((rows * orb, 2 * orbitals), BF16), ((rows * orb, orbitals), BF16)]
            + [((rows * orb, step), F32)] * 2
            + [((count, len(targets) * col_width if last else 128), F32)],
            9 * rows * orb * orbitals * col_width * len(targets),
        )

    blocks = [complete(pairs, True) for pairs in sent[:-1]]
    sums = []
    for v in range(own - 1):
        core, *sums = adjoint(v, list(range(cols)), sums, [((count, rank), F32)], False)
    sent[-1][1:], core = lax.optimization_barrier((sent[-1][1:], core))
    blocks.append(complete(sent[-1], False))
    even, odd, *sums = adjoint(own - 1, list(range(cols)), sums, [((rows // 2, own, rank), F32)] * 2, True)
    parts = sums[:1]
    for k in range(1, cols):
        parts.append(lax.ppermute(sums[k], "col", [(j, (j + k) % cols) for j in range(cols)]))
    core = even + across(odd, 1)
    many = rows // 2
    while many > 1:
        many //= 2
        if many == rows // 4:
            mine, core = lax.optimization_barrier((mine, core))
        core = core[:many] + across(core[many:], 2 * many)
    core_gradient = core[0]

    (factor_part,) = kernel_call(
        functools.partial(factor_kernel, dims),
        "factor",
        index,
        [stacked, mine, every],
        [((orb, col_width), F32)],
        [],
        12 * orbitals * rank * col_width,
    )
    factor_gradient = 4.0 * (factor_part - sum(parts[1:], parts[0]))
    return core_gradient, factor_gradient


def solution(mesh):
    placed = (P(("row", "col"), None, None), P(("row", "col"), None), P(("row", "col"), None))
    return jax.shard_map(
        on_device,
        mesh=mesh,
        in_specs=placed,
        out_specs=(P(("row", "col"), None), P("row", "col")),
        check_vma=False,
    )
```

```python
import functools

import jax
import jax.numpy as jnp
from jax import lax
from jax.experimental import pallas as pl
from jax.experimental.pallas import tpu as pltpu
from jax.sharding import PartitionSpec as P

F32 = jnp.float32
BF16 = jnp.bfloat16
VMEM_LIMIT = 32 * 1024 * 1024


def split(a):
    high = a.astype(BF16)
    return high, (a - high.astype(F32)).astype(BF16)


def dot3(a, b):
    both = functools.partial(jnp.dot, preferred_element_type=F32)
    return both(a[0], b[0]) + both(a[0], b[1]) + both(a[1], b[0])


def dot_stacked(left, rows_ref, span):
    both = functools.partial(jnp.dot, preferred_element_type=F32)
    return both(left[0], rows_ref[:, span]) + both(left[1], rows_ref[: rows_ref.shape[0] // 2, span])


def transposed_left(rows_ref, columns):
    orbitals = rows_ref.shape[0] // 2
    high = rows_ref[:orbitals, columns].T
    return jnp.concatenate([high, high], axis=1), rows_ref[orbitals:, columns].T


def width_of(extent, most):
    return most if extent % most == 0 else extent


def put_rows(ref, start, values, unit, columns):
    height = values.shape[0]
    if height % unit == 0:
        ref[pl.ds(pl.multiple_of(start, unit), height), columns] = values
    else:
        for i in range(height):
            ref[pl.ds(start + i, 1), columns] = values[i : i + 1]


def assemble_kernel(dims, places, index_ref, *refs):
    rows, cols, own, held, rank = dims
    pieces = refs[: len(places)]
    rows_ref, mine_ref, group_ref, all_ref, core_ref, strip_ref, *more = refs[len(places) :]
    orbitals = rows * cols * held
    r = index_ref[0]
    c = index_ref[1]
    packed = pieces[0].shape[1] - rank
    per_row = rank // packed
    lanes = strip_ref.shape[2]
    orb = cols * held
    row_width = rank // rows
    col_width = rank // cols

    def place_of(column):
        return lax.rem(column // col_width + cols - c, cols) * col_width + lax.rem(column, col_width)

    seen = 0
    for piece, (mask, first, many) in zip(pieces, places):
        row = lax.bitwise_xor(r, mask)
        for k in range(many):
            line = lax.rem(c + cols - (first + k), cols)
            start = row * orb + line * held
            for m in range(cols):
                source = pl.ds(pl.multiple_of(lax.rem(c + m, cols) * col_width, col_width), col_width)
                target = slice(m * col_width, (m + 1) * col_width)
                values = piece[k * held : (k + 1) * held, source]
                if more:
                    put_rows(more[0], start, values, 8, target)
                else:
                    high, low = split(values)
                    put_rows(rows_ref, start, high, 16, target)
                    put_rows(rows_ref, orbitals + start, low, 16, target)
                if mask == 0:
                    put_rows(mine_ref, line * held, values, 8, target)
        taken = many * own
        for h in range(packed // lanes):
            strip_ref[h, : many * held, :] = piece[:, rank + h * lanes : rank + (h + 1) * lanes]
            for j in range(per_row):
                at = pl.ds(pl.multiple_of(place_of(jnp.int32(j * packed + h * lanes)), lanes), lanes)
                all_ref[seen : seen + taken, at] = strip_ref[h, pl.ds(j, taken, stride=per_row), :]
        if first == 0:
            group_ref[mask * own : (mask + 1) * own, :] = all_ref[seen : seen + own, :]
        seen += taken
    if more:
        rows_ref[:orbitals, :], rows_ref[orbitals:, :] = split(more[0][...])

    block = pl.ds(pl.multiple_of(place_of(r * row_width), row_width), row_width)
    left = transposed_left(rows_ref, block)
    weights = split(group_ref[:, block])
    step = width_of(rank, 512)
    for n in range(0, rank, step):
        gram = dot_stacked(left, rows_ref, slice(n, n + step))
        core_ref[:, n : n + step] = dot3(weights, split(gram * gram))


def adjoint_kernel(dims, v, targets, last, index_ref, *refs):
    rows, cols, own, held, rank = dims
    blocks = rows // 2 + (1 if v < own - 1 else rows // 2)
    vector_refs = refs[:blocks]
    rows_in_ref, mine_ref, group_ref, core_ref, *refs = refs[blocks:]
    before = refs[: len(targets)] if v else None
    refs = refs[len(targets) :] if v else refs
    outs = refs[:2] if last else refs[:1]
    sums = refs[len(outs) : len(outs) + len(targets)]
    left_high, left_low, even_ref, odd_ref, rows_ref = refs[len(outs) + len(targets) :]
    r = index_ref[0]
    c = index_ref[1]
    orb = cols * held
    col_width = rank // cols
    step = even_ref.shape[1]
    stages = (even_ref, odd_ref)
    core = pl.multiple_of(lax.rem(r, 2) * orb, orb)
    for i in range(rows):
        if i % 2 == 0:
            values = vector_refs[i // 2][pl.ds(core, orb), :]
        elif v < own - 1:
            values = vector_refs[-1][i // 2 * orb : (i // 2 + 1) * orb]
        else:
            values = vector_refs[rows // 2 + i // 2][...]
        part = slice(i * orb, (i + 1) * orb)
        high, low = split(values)
        left_high[part, :], left_low[part, :] = jnp.concatenate([high, high], axis=1), low
    order = [(t, m) for t in range(len(targets)) for m in range(0, col_width, step)]

    def publish(target, values_ref, base):
        at = pl.ds(pl.multiple_of(lax.rem(c + target, cols) * col_width, col_width), col_width)
        for i in range(rows):
            outs[i % 2][i // 2, :, at] = values_ref[i * own : (i + 1) * own, base : base + col_width]

    def finish(n):
        t, m = order[n]
        span = slice(targets[t] * col_width + m, targets[t] * col_width + m + step)
        place = slice(t * col_width + m, t * col_width + m + step)
        kept = rows_ref if last else outs[0]
        kept[:, place] = core_ref[:, span]
        mine = mine_ref[:, span]
        total = before[t][:, m : m + step] if v else jnp.zeros_like(mine)
        for i in range(rows):
            at = i * own + v
            adjoint = stages[n % 2][i * orb : (i + 1) * orb, :]
            projection = jnp.sum(adjoint * mine, axis=0, keepdims=True)
            kept[at : at + 1, place] = core_ref[at : at + 1, span] - projection
            total = total + adjoint * group_ref[at : at + 1, span]
        sums[t][:, m : m + step] = total

    for n, (t, m) in enumerate(order):
        span = slice(targets[t] * col_width + m, targets[t] * col_width + m + step)
        stages[n % 2][...] = dot_stacked((left_high[...], left_low[...]), rows_in_ref, span)
        if n:
            finish(n - 1)
    finish(len(order) - 1)
    if last:
        for t, target in enumerate(targets):
            publish(target, rows_ref, t * col_width)


def factor_kernel(dims, index_ref, rows_ref, mine_ref, all_ref, out_ref):
    rows, cols, own, held, rank = dims
    col_width = rank // cols
    block = slice(0, col_width)
    left = transposed_left(rows_ref, block)
    weight_left = split(all_ref[:, block].T)
    weight_left = jnp.concatenate([weight_left[0], weight_left[0], weight_left[1]], axis=1)
    mine = jnp.concatenate(split(mine_ref[...].T), axis=1)
    orb = cols * held
    total = jnp.zeros((col_width, 2 * orb), F32)
    side = jnp.zeros((col_width, orb), F32)
    step = width_of(rank, 512)
    for n in range(0, rank, step):
        gram = dot_stacked(left, rows_ref, slice(n, n + step))
        weight = split(all_ref[:, n : n + step])
        weight = jnp.concatenate([weight[0], weight[1], weight[0]], axis=0)
        mixed = split(gram * jnp.dot(weight_left, weight, preferred_element_type=F32))
        total = total + jnp.dot(mixed[0], mine[n : n + step], preferred_element_type=F32)
        side = side + jnp.dot(mixed[1], mine[n : n + step, :orb], preferred_element_type=F32)
    out_ref[...] = (total[:, :orb] + total[:, orb:] + side).T


def kernel_call(body, name, index, operands, outs, scratch, flops):
    whole = pl.BlockSpec(memory_space=pltpu.VMEM)
    moved = sum(a.size * a.dtype.itemsize for a in operands)
    return pl.pallas_call(
        body,
        out_shape=tuple(pltpu.VMEM(*out) for out in outs),
        in_specs=[pl.BlockSpec(memory_space=pltpu.SMEM)] + [whole] * len(operands),
        out_specs=(whole,) * len(outs),
        scratch_shapes=[pltpu.VMEM(*held) for held in scratch],
        compiler_params=pltpu.CompilerParams(vmem_limit_bytes=VMEM_LIMIT),
        cost_estimate=pl.CostEstimate(flops=flops, bytes_accessed=moved, transcendentals=0),
        name=name,
    )(index, *(pltpu.with_memory_space_constraint(a, pltpu.VMEM) for a in operands))


def on_device(vectors, factor, weights):
    rows = lax.axis_size("row")
    cols = lax.axis_size("col")
    r = lax.axis_index("row")
    c = lax.axis_index("col")
    own, orbitals = vectors.shape[:2]
    held, rank = factor.shape
    orb = orbitals // rows
    col_width = rank // cols
    count = rows * own
    dims = (rows, cols, own, held, rank)
    index = jnp.stack([r, c]).astype(jnp.int32)

    def across(a, mask):
        return lax.ppermute(a, "row", [(i, i ^ mask) for i in range(rows)])

    def pairs_of(v):
        starts = [((r ^ mask) // 2) * 2 * orb for mask in range(0, rows, 2)]
        return [lax.dynamic_slice(vectors, (v, start, 0), (1, 2 * orb, orbitals))[0] for start in starts]

    def send(pairs):
        return pairs[:1] + [across(pair, 2 * m) for m, pair in enumerate(pairs) if m]

    def complete(pairs, together):
        passed = [lax.dynamic_slice_in_dim(pair, (1 - r % 2) * orb, orb, 0) for pair in pairs]
        return pairs + [across(part, 1) for part in ([jnp.concatenate(passed, axis=0)] if together else passed)]

    block = jnp.concatenate([factor, weights.reshape(held, own * rank // held)], axis=1)
    line = [block]
    for k in range(1, cols):
        line.append(lax.ppermute(block, "col", [(j, (j + k) % cols) for j in range(cols)]))
    first = send(pairs_of(0))
    line, first, vectors = lax.optimization_barrier((jnp.concatenate(line, axis=0), first, vectors))

    later = [pairs_of(v) for v in range(1, own)]
    whole = [(line, 0, 0, cols)]
    other = [across(line, 1)]
    if rows == 8:
        half = cols // 2
        one, two = across(line, 2), across(line, 4)
        give, take, later = lax.optimization_barrier((two[: half * held], one[half * held :], later))
        whole += [(one, 2, 0, cols), (two, 4, 0, cols)]
        other += [across(one, 1), across(two, 1)]
        whole += [(across(give, 2), 6, 0, half), (across(take, 4), 6, half, cols - half)]
    else:
        whole += [(across(line, m), m, 0, cols) for m in range(2, rows, 2)]
    later, other[0] = lax.optimization_barrier((later, other[0]))
    other += [across(part[0], 1) for part in whole[len(other) :]]
    whole += [(part, mask + 1, start, many) for part, (_, mask, start, many) in zip(other, whole)]
    sent = [first] + [send(pairs) for pairs in later]
    stacked, mine, group, every, core = kernel_call(
        functools.partial(assemble_kernel, dims, [part[1:] for part in whole]),
        "assemble",
        index,
        [part[0] for part in whole],
        [
            ((2 * orbitals, rank), BF16),
            ((orb, rank), F32),
            ((count, rank), F32),
            ((count * cols, rank), F32),
            ((count, rank), F32),
        ],
        [((own * rank // held // 128, orb, 128), F32)] + ([] if held % 16 == 0 else [((orbitals, rank), F32)]),
        21 * orbitals * rank * rank // rows,
    )

    step = width_of(col_width, 512)

    def adjoint(v, targets, extra, outs, last):
        return kernel_call(
            functools.partial(adjoint_kernel, dims, v, targets, last),
            "adjoint",
            index,
            [*blocks[v], stacked, mine, group, core, *extra],
            outs + [((orb, col_width), F32)] * len(targets),
            [((rows * orb, 2 * orbitals), BF16), ((rows * orb, orbitals), BF16)]
            + [((rows * orb, step), F32)] * 2
            + [((count, len(targets) * col_width if last else 128), F32)],
            9 * rows * orb * orbitals * col_width * len(targets),
        )

    blocks = [complete(pairs, True) for pairs in sent[:-1]]
    sums = []
    for v in range(own - 1):
        core, *sums = adjoint(v, list(range(cols)), sums, [((count, rank), F32)], False)
    sent[-1][1:], core = lax.optimization_barrier((sent[-1][1:], core))
    blocks.append(complete(sent[-1], False))
    even, odd, *sums = adjoint(own - 1, list(range(cols)), sums, [((rows // 2, own, rank), F32)] * 2, True)
    parts = sums[:1]
    for k in range(1, cols):
        parts.append(lax.ppermute(sums[k], "col", [(j, (j + k) % cols) for j in range(cols)]))
    core = even + across(odd, 1)
    many = rows // 2
    while many > 1:
        many //= 2
        if many == rows // 4:
            mine, core = lax.optimization_barrier((mine, core))
        core = core[:many] + across(core[many:], 2 * many)
    core_gradient = core[0]

    (factor_part,) = kernel_call(
        functools.partial(factor_kernel, dims),
        "factor",
        index,
        [stacked, mine, every],
        [((orb, col_width), F32)],
        [],
        12 * orbitals * rank * col_width,
    )
    factor_gradient = 4.0 * (factor_part - sum(parts[1:], parts[0]))
    return core_gradient, factor_gradient


def solution(mesh):
    placed = (P(("row", "col"), None, None), P(("row", "col"), None), P(("row", "col"), None))
    return jax.shard_map(
        on_device,
        mesh=mesh,
        in_specs=placed,
        out_specs=(P(("row", "col"), None), P("row", "col")),
        check_vma=False,
    )
```
